32 devices in a mesh: space: 16 (over z, x, core), shot: 2 (over y).
Axes of the slice: x: 2, y: 2, z: 4, core: 2. Of those that a mesh axis runs over, the one named last changes fastest.
Arguments:
- courant: float32 [256, 64, 128], P('space'), may hold values from 0.15 to 0.42
- p_current: float32 [2, 256, 64, 128], P('shot', 'space'), may hold values from -6 to 6
- p_later: float32 [2, 256, 64, 128], P('shot', 'space'), may hold values from -6 to 6
- q_current: float32 [2, 256, 64, 128], P('shot', 'space'), may hold values from -6 to 6
- q_later: float32 [2, 256, 64, 128], P('shot', 'space'), may hold values from -6 to 6
- wavelet: float32 [2, 6], P('shot'), may hold values from -24 to 24
- source_cell: int32 [2], P('shot'), may hold values from 0 to 2097151
- receiver_cells: int32 [2, 256], P('shot'), may hold values from 0 to 2097151
- residual_data: float32 [2, 6, 256], P('shot'), may hold values from -6 to 6
Outputs:
- gradient: float32 [256, 64, 128], P('space', 'shot')
- q_final: float32 [2, 256, 64, 128], P('shot', 'space')
The draws below stay inside these ranges and needn't reach their ends.
Inputs may be any that keep to these rules, and one draw needn't show every extreme that they name: `source_cell`: a flat cell index of the whole grid. `receiver_cells`: flat cell indices of the whole grid; cells may repeat.
All inputs are finite; a program needn't handle non-finite values.
Results may differ from the reference program's by a relative error of at most 0.0003.
Values sent between devices are 32-bit elements; how exact they have to be, the bound alone decides.
A program may use at most 64 MiB of HBM per device.

```python
import math
import jax
import jax.numpy as jnp
from jax import lax

NY = 64
NZ = 128
STEPS = 6
REC = 256
NX = 256
SHOTS = 2


def set_ends(result, key, low, high):
    spot = [jax.random.randint(jax.random.fold_in(key, axis), (), 0, length) for axis, length in enumerate(result.shape)]
    longest = result.shape.index(max(result.shape))
    next_to = spot[:longest] + [(spot[longest] + 1) % result.shape[longest]] + spot[longest + 1:]
    return result.at[tuple(spot)].set(low).at[tuple(next_to)].set(high)


def steps_of(rng, shape, shards, low, top_value):
    level, own = 1.0, jax.random.fold_in(rng, 6)
    for dim, blocks in shards:
        steps = jnp.exp(jax.random.uniform(jax.random.fold_in(own, dim), (blocks,), jnp.float32, low / len(shards), top_value / len(shards)))
        level = level * jnp.repeat(steps, shape[dim] // blocks).reshape([-1 if axis == dim else 1 for axis in range(len(shape))])
    return level


def scatter_about(rng, shape, scale, reach, cuts=(), held_as=jnp.bfloat16):
    drawn = jax.random.normal(rng, shape, jnp.float32) * scale
    if len(cuts) > 0:
        drawn = steps_of(rng, shape, cuts, -0.22, 0.18) * drawn
    return jnp.clip(drawn, min=-reach, max=reach).astype(held_as)


def setup_inputs(seed: int = 0) -> dict:
    arg_keys = jax.random.split(jax.random.key(seed), 10)
    courant = jnp.clip(jnp.exp(math.log(0.42) - 1.0296193 * jax.random.uniform(arg_keys[0], (NX, NY, NZ), jnp.float32) ** steps_of(arg_keys[0], (NX, NY, NZ), ((0, 16),), -0.2, 0.2)), 0.15, 0.42)
    p_current = scatter_about(arg_keys[1], (SHOTS, NX, NY, NZ), 1.0, 6.0, ((0, 2), (1, 16)), jnp.float32)
    p_later = scatter_about(arg_keys[2], (SHOTS, NX, NY, NZ), 1.0, 6.0, ((0, 2), (1, 16)), jnp.float32)
    q_current = scatter_about(arg_keys[3], (SHOTS, NX, NY, NZ), 1.0, 6.0, ((0, 2), (1, 16)), jnp.float32)
    q_later = scatter_about(arg_keys[4], (SHOTS, NX, NY, NZ), 1.0, 6.0, ((0, 2), (1, 16)), jnp.float32)
    wavelet = scatter_about(arg_keys[5], (SHOTS, STEPS), 4.0, 24.0, ((0, 2),), jnp.float32)
    source_cell = jax.random.randint(arg_keys[6], (SHOTS,), 0, NX * NY * NZ).astype(jnp.int32)
    receiver_cells = set_ends(jax.random.randint(arg_keys[7], (SHOTS, REC), 0, NX * NY * NZ), jax.random.fold_in(arg_keys[7], 1), 0, (NX * NY * NZ) - 1).astype(jnp.int32)
    residual_data = scatter_about(arg_keys[8], (SHOTS, STEPS, REC), 1.0, 6.0, ((0, 2),), jnp.float32)
    return dict(courant=courant, p_current=p_current, p_later=p_later, q_current=q_current, q_later=q_later, wavelet=wavelet, source_cell=source_cell, receiver_cells=receiver_cells, residual_data=residual_data)


coefs = (-205.0 / 72.0, 8.0 / 5.0, -1.0 / 5.0, 8.0 / 315.0, -1.0 / 560.0)


def laplace_rows(field):
    extent = field.shape[0]
    core = field[4:extent - 4]
    total = 3.0 * coefs[0] * core
    for j in range(1, 5):
        total = total + coefs[j] * (field[4 + j:extent - 4 + j] + field[4 - j:extent - 4 - j])
    width_y = core.shape[1]
    padded_y = jnp.pad(core, ((0, 0), (4, 4), (0, 0)))
    for j in range(1, 5):
        total = total + coefs[j] * (padded_y[:, 4 + j:4 + j + width_y] + padded_y[:, 4 - j:4 - j + width_y])
    width_z = core.shape[2]
    padded_z = jnp.pad(core, ((0, 0), (0, 0), (4, 4)))
    for j in range(1, 5):
        total = total + coefs[j] * (padded_z[:, :, 4 + j:4 + j + width_z] + padded_z[:, :, 4 - j:4 - j + width_z])
    return total


def laplace_whole(field):
    return laplace_rows(jnp.pad(field, ((4, 4), (0, 0), (0, 0))))


def inject_cells(field, cells, values):
    flat = field.reshape(-1)
    flat = flat.at[cells.astype(jnp.int32)].add(values)
    return flat.reshape(field.shape)


def reference(courant, p_current, p_later, q_current, q_later, wavelet, source_cell, receiver_cells, residual_data):
    speed2 = courant * courant

    def one_shot(total, items):
        pc, pn, qc, qn, wave, source, receivers, residual = items
        grad = jnp.zeros(pc.shape, jnp.float32)
        for k in range(STEPS):
            lp = laplace_whole(pc)
            lq = laplace_whole(qc)
            grad = grad + qc * lp
            p_new = inject_cells(2.0 * pc - pn + speed2 * lp, source[None], wave[k][None])
            q_new = inject_cells(2.0 * qc - qn + speed2 * lq, receivers, residual[k])
            pn, pc = pc, p_new
            qn, qc = qc, q_new
        return total + grad, qc

    start = jnp.zeros(courant.shape, jnp.float32)
    summed, q_final = lax.scan(one_shot, start, (p_current, p_later, q_current, q_later, wavelet, source_cell, receiver_cells, residual_data))
    gradient = summed * (1.0 / (STEPS * SHOTS))
    return gradient, q_final
```

```python
import functools

import jax
import jax.numpy as jnp
import ml_dtypes
import numpy as np
from jax import lax
from jax.experimental import pallas as pl
from jax.experimental.pallas import tpu as pltpu
from jax.sharding import PartitionSpec as P

STEPS = 6
WIDTH = 4
PAD = 8

coefs = (-205.0 / 72.0, 8.0 / 5.0, -1.0 / 5.0, 8.0 / 315.0, -1.0 / 560.0)


def band(depth):
    whole = np.zeros((depth, depth), np.float32)
    for j in range(1, WIDTH + 1):
        whole += np.float32(coefs[j]) * (np.eye(depth, k=j, dtype=np.float32) + np.eye(depth, k=-j, dtype=np.float32))
    high = whole.astype(ml_dtypes.bfloat16)
    low = (whole - high.astype(np.float32)).astype(ml_dtypes.bfloat16)
    return np.block([[high, low], [high, np.zeros_like(high)]])


def split(value, terms):
    parts = []
    for _ in range(terms):
        part = value.astype(jnp.bfloat16)
        parts.append(part)
        value = value - part.astype(jnp.float32)
    return parts


def kernel(
    count, shots,
    courant, p_current, p_later, q_current, q_later, wavelet, source, receivers, residual, matrix,
    gradient, q_final,
    p_ext, q_ext, speed2, grad, spot, inject, others,
    load_sem, send_sem, recv_sem, share_send, share_recv,
):
    rows, ny, nz = speed2.shape
    me = lax.axis_index("space")
    shot = lax.axis_index("shot")
    odd = lax.rem(me, 2)
    exts = (p_ext, q_ext)
    currents = (p_current, q_current)
    ys = pl.ds(PAD, ny)

    def neighbour(side):
        return me - 1 + 2 * side

    def exists(side):
        return jnp.logical_and(neighbour(side) >= 0, neighbour(side) < count)

    def halo_copy(f, k, side):
        dst = exts[f].at[k + 1, pl.ds((1 - side) * (rows + WIDTH), WIDTH), ys]
        if isinstance(k, int) and k == 0:
            src = currents[f].at[0, pl.ds(side * (rows - WIDTH), WIDTH)]
        else:
            src = exts[f].at[k + 1, pl.ds(WIDTH + side * (rows - WIDTH), WIDTH), ys]
        return pltpu.make_async_remote_copy(
            src_ref=src, dst_ref=dst,
            send_sem=send_sem.at[f, k, side], recv_sem=recv_sem.at[f, k, side],
            device_id={"space": neighbour(side)}, device_id_type=pl.DeviceIdType.MESH,
        )

    def halo_wait(f, k, side):
        @pl.when(exists(side))
        def _():
            here = exts[f].at[k + 1, pl.ds(side * (rows + WIDTH), WIDTH), ys]
            pltpu.make_async_remote_copy(
                src_ref=here, dst_ref=here,
                send_sem=send_sem.at[f, k, 1 - side], recv_sem=recv_sem.at[f, k, 1 - side],
                device_id={"space": neighbour(side)}, device_id_type=pl.DeviceIdType.MESH,
            ).wait_recv()

    def halo_send(f, k, side):
        @pl.when(exists(side))
        def _():
            halo_copy(f, k, side).start()

    slow, fast = odd, 1 - odd

    loads = [
        pltpu.make_async_copy(courant, speed2, load_sem.at[0]),
        pltpu.make_async_copy(p_current.at[0], p_ext.at[1, pl.ds(WIDTH, rows), ys], load_sem.at[1]),
        pltpu.make_async_copy(q_current.at[0], q_ext.at[1, pl.ds(WIDTH, rows), ys], load_sem.at[2]),
        pltpu.make_async_copy(p_later.at[0], p_ext.at[0, pl.ds(WIDTH, rows), ys], load_sem.at[3]),
        pltpu.make_async_copy(q_later.at[0], q_ext.at[0, pl.ds(WIDTH, rows), ys], load_sem.at[4]),
    ]
    for load in loads:
        load.start()

    barrier = pltpu.get_barrier_semaphore()
    for side in (0, 1):
        @pl.when(exists(side))
        def _():
            pl.semaphore_signal(
                barrier, inc=1, device_id={"space": neighbour(side)}, device_id_type=pl.DeviceIdType.MESH
            )
    for d in range(1, shots):
        pl.semaphore_signal(
            barrier, inc=1, device_id={"shot": lax.rem(shot + d, shots)}, device_id_type=pl.DeviceIdType.MESH
        )
    pl.semaphore_wait(
        barrier, exists(0).astype(jnp.int32) + exists(1).astype(jnp.int32) + (shots - 1)
    )
    for f in (0, 1):
        for side in (slow, fast):
            halo_send(f, 0, side)

    for ext in exts:
        edge = jnp.zeros((ext.shape[0] - 1, rows, PAD, nz), jnp.float32)
        ext[1:, WIDTH:WIDTH + rows, 0:PAD, :] = edge
        ext[1:, WIDTH:WIDTH + rows, PAD + ny:PAD + ny + PAD, :] = edge
        outside = jnp.zeros((ext.shape[0] - 1, WIDTH, ny, nz), jnp.float32)
        for side in (0, 1):
            @pl.when(jnp.logical_not(exists(side)))
            def _():
                ext[1:, side * (rows + WIDTH):side * (rows + WIDTH) + WIDTH, PAD:PAD + ny, :] = outside

    shift = nz.bit_length() - 1
    cells = receivers[...]
    cell_row = lax.shift_right_logical(cells, shift) - me * (rows * ny)
    cell_column = jnp.bitwise_and(cells, nz - 1)
    column_hit = lax.broadcasted_iota(jnp.int32, (nz, cells.shape[1]), 0) == cell_column
    values = jnp.concatenate(
        [jnp.where(column_hit, residual[0, k:k + 1, :], 0.0) for k in range(STEPS)], axis=0
    )
    value_parts = split(values, 3)
    block = WIDTH * ny
    for c in range(rows // WIDTH):
        ids = lax.broadcasted_iota(jnp.int32, (block, cells.shape[1]), 0) + c * block
        row_hit = jnp.where(ids == cell_row, 1.0, 0.0).astype(jnp.bfloat16)
        total = None
        for part in value_parts:
            term = lax.dot_general(
                row_hit, part, (((1,), (1,)), ((), ())), preferred_element_type=jnp.float32
            )
            total = term if total is None else total + term
        for k in range(STEPS):
            inject[k, c * WIDTH:(c + 1) * WIDTH] = total[:, k * nz:(k + 1) * nz].reshape(WIDTH, ny, nz)
        flat = (
            (lax.broadcasted_iota(jnp.int32, (WIDTH, ny, nz), 0) + (me * rows + c * WIDTH)) * (ny * nz)
            + lax.broadcasted_iota(jnp.int32, (WIDTH, ny, nz), 1) * nz
            + lax.broadcasted_iota(jnp.int32, (WIDTH, ny, nz), 2)
        )
        spot[c * WIDTH:(c + 1) * WIDTH] = jnp.where(flat == source[0], 1.0, 0.0)
    grad[...] = jnp.zeros_like(grad)
    for load in loads:
        load.wait()
    speed2[...] = speed2[...] * speed2[...]

    def laplace(ext, t, r0):
        here = pl.ds(r0 + WIDTH, WIDTH)
        core = ext[t, here, ys, :]
        pair = jnp.concatenate(split(core, 2), axis=-1).reshape(WIDTH * ny, 2 * nz)
        along_z = jnp.dot(pair, matrix[...], preferred_element_type=jnp.float32)
        total = (along_z[:, :nz] + along_z[:, nz:]).reshape(WIDTH, ny, nz) + 3.0 * coefs[0] * core
        for j in range(1, WIDTH + 1):
            total = total + coefs[j] * (
                (ext[t, pl.ds(r0 + WIDTH + j, WIDTH), ys, :] + ext[t, pl.ds(r0 + WIDTH - j, WIDTH), ys, :])
                + (ext[t, here, pl.ds(PAD + j, ny), :] + ext[t, here, pl.ds(PAD - j, ny), :])
            )
        return core, total

    def p_chunk(k, r0, last):
        core, lap = laplace(p_ext, k + 1, r0)
        own, here = pl.ds(r0, WIDTH), pl.ds(r0 + WIDTH, WIDTH)
        grad[own] += q_ext[k + 1, here, ys, :] * lap
        if not last:
            p_ext[k + 2, here, ys, :] = (
                2.0 * core - p_ext[k, here, ys, :] + speed2[own] * lap + wavelet[0, k] * spot[own]
            )

    def q_chunk(k, r0, last):
        core, lap = laplace(q_ext, k + 1, r0)
        own, here = pl.ds(r0, WIDTH), pl.ds(r0 + WIDTH, WIDTH)
        new = 2.0 * core - q_ext[k, here, ys, :] + speed2[own] * lap + inject[k, own]
        if last:
            q_final[0, own] = new
        else:
            q_ext[k + 2, here, ys, :] = new

    chunks = (p_chunk, q_chunk)

    def step(k, last=False, after_inner=None, after_side=None):
        for f in (0, 1):
            for c in range(1, rows // WIDTH - 1):
                chunks[f](k, c * WIDTH, last)
            if f == 0 and after_inner is not None:
                after_inner()
            for side in (fast, slow):
                halo_wait(f, k, side)
                chunks[f](k, side * (rows - WIDTH), last)
                if not last:
                    halo_send(f, k + 1, side)
                elif f == 0:
                    after_side(side)

    def loop(k, carry):
        step(k)
        return carry

    lax.fori_loop(0, STEPS - 1, loop, 0)

    share = ny // shots

    def share_copy(d, part, start, length):
        target = lax.rem(shot + d, shots)
        return pltpu.make_async_remote_copy(
            src_ref=grad.at[pl.ds(start, length), pl.ds(pl.multiple_of(target * share, share), share)],
            dst_ref=others.at[d - 1, pl.ds(start, length)],
            send_sem=share_send.at[d - 1, part], recv_sem=share_recv.at[d - 1, part],
            device_id={"shot": target}, device_id_type=pl.DeviceIdType.MESH,
        )

    def inner_parts(d):
        return share_copy(d, 2, WIDTH, rows - 2 * WIDTH)

    def side_part(d, side):
        return share_copy(d, side, side * (rows - WIDTH), WIDTH)

    def send_inner():
        for d in range(1, shots):
            inner_parts(d).start()

    def send_side(side):
        for d in range(1, shots):
            side_part(d, side).start()

    step(STEPS - 1, True, send_inner, send_side)

    for d in range(1, shots):
        inner_parts(d).wait()
        for side in (fast, slow):
            side_part(d, side).wait()
    total = grad[:, pl.ds(pl.multiple_of(shot * share, share), share), :]
    for d in range(1, shots):
        total = total + others[d - 1]
    gradient[...] = total * (1.0 / (STEPS * shots))

    for f in (0, 1):
        for side in (0, 1):
            @pl.when(exists(side))
            def _():
                halo_copy(f, 0, side).wait_send()

                def finish(k, carry):
                    halo_copy(f, k, side).wait_send()
                    return carry

                lax.fori_loop(1, STEPS, finish, 0)


def body(courant, p_current, p_later, q_current, q_later, wavelet, source_cell, receiver_cells, residual_data):
    rows, ny, nz = courant.shape
    count, shots = lax.axis_size("space"), lax.axis_size("shot")
    share = ny // shots
    hbm = pl.BlockSpec(memory_space=pl.ANY)
    vmem = pl.BlockSpec(memory_space=pltpu.VMEM)
    smem = pl.BlockSpec(memory_space=pltpu.SMEM)
    cells = rows * ny * nz
    call = pl.pallas_call(
        functools.partial(kernel, count, shots),
        out_shape=(
            jax.ShapeDtypeStruct((rows, share, nz), jnp.float32),
            jax.ShapeDtypeStruct((1, rows, ny, nz), jnp.float32),
        ),
        in_specs=[hbm] * 5 + [smem, smem, vmem, vmem, vmem],
        out_specs=(vmem, vmem),
        scratch_shapes=[
            pltpu.VMEM((STEPS + 1, rows + 2 * WIDTH, ny + 2 * PAD, nz), jnp.float32),
            pltpu.VMEM((STEPS + 1, rows + 2 * WIDTH, ny + 2 * PAD, nz), jnp.float32),
            pltpu.VMEM((rows, ny, nz), jnp.float32),
            pltpu.VMEM((rows, ny, nz), jnp.float32),
            pltpu.VMEM((rows, ny, nz), jnp.float32),
            pltpu.VMEM((STEPS, rows, ny, nz), jnp.float32),
            pltpu.VMEM((max(shots - 1, 1), rows, share, nz), jnp.float32),
            pltpu.SemaphoreType.DMA((5,)),
            pltpu.SemaphoreType.DMA((2, STEPS, 2)),
            pltpu.SemaphoreType.DMA((2, STEPS, 2)),
            pltpu.SemaphoreType.DMA((max(shots - 1, 1), 3)),
            pltpu.SemaphoreType.DMA((max(shots - 1, 1), 3)),
        ],
        compiler_params=pltpu.CompilerParams(
            collective_id=0, has_side_effects=True, vmem_limit_bytes=44 * 1024 * 1024
        ),
        cost_estimate=pl.CostEstimate(
            flops=2 * STEPS * 40 * cells, bytes_accessed=7 * 4 * cells, transcendentals=0
        ),
    )
    return call(
        courant, p_current, p_later, q_current, q_later, wavelet, source_cell, receiver_cells, residual_data,
        jnp.asarray(band(nz)),
    )


def solution(mesh):
    in_specs = (
        P("space", None, None),
        P("shot", "space", None, None),
        P("shot", "space", None, None),
        P("shot", "space", None, None),
        P("shot", "space", None, None),
        P("shot", None),
        P("shot"),
        P("shot", None),
        P("shot", None, None),
    )
    out_specs = (P("space", "shot", None), P("shot", "space", None, None))
    return jax.shard_map(body, mesh=mesh, in_specs=in_specs, out_specs=out_specs, check_vma=False)
```

```python
import functools

import jax
import jax.numpy as jnp
from jax import lax
from jax.experimental import pallas as pl
from jax.experimental.pallas import tpu as pltpu
from jax.sharding import PartitionSpec as P

STEPS = 6
WIDTH = 4
PAD = 8

coefs = (-205.0 / 72.0, 8.0 / 5.0, -1.0 / 5.0, 8.0 / 315.0, -1.0 / 560.0)


def band(depth):
    apart = jnp.abs(
        lax.broadcasted_iota(jnp.int32, (depth, depth), 0) - lax.broadcasted_iota(jnp.int32, (depth, depth), 1)
    )
    whole = jnp.zeros((depth, depth), jnp.float32)
    for j in range(1, WIDTH + 1):
        whole = jnp.where(apart == j, coefs[j], whole)
    high, low = split(whole, 2)
    return jnp.concatenate(
        [jnp.concatenate([high, low], axis=1), jnp.concatenate([high, jnp.zeros_like(high)], axis=1)], axis=0
    )


def split(value, terms):
    parts = []
    for _ in range(terms):
        part = value.astype(jnp.bfloat16)
        parts.append(part)
        value = value - part.astype(jnp.float32)
    return parts


def kernel(
    count, shots,
    courant, p_current, p_later, q_current, q_later, wavelet, source, receivers, residual,
    gradient, q_final,
    p_ext, q_ext, speed2, grad, spot, inject, others, matrix, summed,
    load_sem, out_sem, send_sem, recv_sem, share_send, share_recv,
):
    rows, ny, nz = speed2.shape
    me = lax.axis_index("space")
    shot = lax.axis_index("shot")
    odd = lax.rem(me, 2)
    exts = (p_ext, q_ext)
    currents = (p_current, q_current)
    ys = pl.ds(PAD, ny)

    def neighbour(side):
        return me - 1 + 2 * side

    def exists(side):
        return jnp.logical_and(neighbour(side) >= 0, neighbour(side) < count)

    def halo_copy(f, k, side):
        dst = exts[f].at[k + 1, pl.ds((1 - side) * (rows + WIDTH), WIDTH), ys]
        if isinstance(k, int) and k == 0:
            src = currents[f].at[0, pl.ds(side * (rows - WIDTH), WIDTH)]
        else:
            src = exts[f].at[k + 1, pl.ds(WIDTH + side * (rows - WIDTH), WIDTH), ys]
        return pltpu.make_async_remote_copy(
            src_ref=src, dst_ref=dst,
            send_sem=send_sem.at[f, k, side], recv_sem=recv_sem.at[f, k, side],
            device_id={"space": neighbour(side)}, device_id_type=pl.DeviceIdType.MESH,
        )

    def halo_wait(f, k, side):
        @pl.when(exists(side))
        def _():
            here = exts[f].at[k + 1, pl.ds(side * (rows + WIDTH), WIDTH), ys]
            pltpu.make_async_remote_copy(
                src_ref=here, dst_ref=here,
                send_sem=send_sem.at[f, k, 1 - side], recv_sem=recv_sem.at[f, k, 1 - side],
                device_id={"space": neighbour(side)}, device_id_type=pl.DeviceIdType.MESH,
            ).wait_recv()

    def halo_send(f, k, side):
        @pl.when(exists(side))
        def _():
            halo_copy(f, k, side).start()

    slow, fast = odd, 1 - odd

    loads = [
        pltpu.make_async_copy(courant, speed2, load_sem.at[0]),
        pltpu.make_async_copy(p_current.at[0], p_ext.at[1, pl.ds(WIDTH, rows), ys], load_sem.at[1]),
        pltpu.make_async_copy(q_current.at[0], q_ext.at[1, pl.ds(WIDTH, rows), ys], load_sem.at[2]),
        pltpu.make_async_copy(p_later.at[0], p_ext.at[0, pl.ds(WIDTH, rows), ys], load_sem.at[3]),
        pltpu.make_async_copy(q_later.at[0], q_ext.at[0, pl.ds(WIDTH, rows), ys], load_sem.at[4]),
    ]
    for load in loads:
        load.start()

    barrier = pltpu.get_barrier_semaphore()
    for side in (0, 1):
        @pl.when(exists(side))
        def _():
            pl.semaphore_signal(
                barrier, inc=1, device_id={"space": neighbour(side)}, device_id_type=pl.DeviceIdType.MESH
            )
    for d in range(1, shots):
        pl.semaphore_signal(
            barrier, inc=1, device_id={"shot": lax.rem(shot + d, shots)}, device_id_type=pl.DeviceIdType.MESH
        )
    pl.semaphore_wait(
        barrier, exists(0).astype(jnp.int32) + exists(1).astype(jnp.int32) + (shots - 1)
    )
    for f in (0, 1):
        for side in (slow, fast):
            halo_send(f, 0, side)

    matrix[...] = band(nz)
    for ext in exts:
        edge = jnp.zeros((ext.shape[0] - 1, rows, PAD, nz), jnp.float32)
        ext[1:, WIDTH:WIDTH + rows, 0:PAD, :] = edge
        ext[1:, WIDTH:WIDTH + rows, PAD + ny:PAD + ny + PAD, :] = edge
        outside = jnp.zeros((ext.shape[0] - 1, WIDTH, ny, nz), jnp.float32)
        for side in (0, 1):
            @pl.when(jnp.logical_not(exists(side)))
            def _():
                ext[1:, side * (rows + WIDTH):side * (rows + WIDTH) + WIDTH, PAD:PAD + ny, :] = outside

    shift = nz.bit_length() - 1
    cells = receivers[...]
    cell_row = lax.shift_right_logical(cells, shift) - me * (rows * ny)
    cell_column = jnp.bitwise_and(cells, nz - 1)
    column_hit = lax.broadcasted_iota(jnp.int32, (nz, cells.shape[1]), 0) == cell_column
    values = jnp.concatenate(
        [jnp.where(column_hit, residual[k], 0.0) for k in range(STEPS)], axis=0
    )
    value_parts = split(values, 3)
    block = WIDTH * ny
    for c in range(rows // WIDTH):
        ids = lax.broadcasted_iota(jnp.int32, (block, cells.shape[1]), 0) + c * block
        row_hit = jnp.where(ids == cell_row, 1.0, 0.0).astype(jnp.bfloat16)
        total = None
        for part in value_parts:
            term = lax.dot_general(
                row_hit, part, (((1,), (1,)), ((), ())), preferred_element_type=jnp.float32
            )
            total = term if total is None else total + term
        for k in range(STEPS):
            inject[k, c * WIDTH:(c + 1) * WIDTH] = total[:, k * nz:(k + 1) * nz].reshape(WIDTH, ny, nz)
        flat = (
            (lax.broadcasted_iota(jnp.int32, (WIDTH, ny, nz), 0) + (me * rows + c * WIDTH)) * (ny * nz)
            + lax.broadcasted_iota(jnp.int32, (WIDTH, ny, nz), 1) * nz
            + lax.broadcasted_iota(jnp.int32, (WIDTH, ny, nz), 2)
        )
        spot[c * WIDTH:(c + 1) * WIDTH] = jnp.where(flat == source[0], 1.0, 0.0)
    grad[...] = jnp.zeros_like(grad)
    for load in loads:
        load.wait()
    speed2[...] = speed2[...] * speed2[...]

    def laplace(ext, t, r0):
        here = pl.ds(r0 + WIDTH, WIDTH)
        core = ext[t, here, ys, :]
        pair = jnp.concatenate(split(core, 2), axis=-1).reshape(WIDTH * ny, 2 * nz)
        along_z = jnp.dot(pair, matrix[...], preferred_element_type=jnp.float32)
        total = (along_z[:, :nz] + along_z[:, nz:]).reshape(WIDTH, ny, nz) + 3.0 * coefs[0] * core
        for j in range(1, WIDTH + 1):
            total = total + coefs[j] * (
                (ext[t, pl.ds(r0 + WIDTH + j, WIDTH), ys, :] + ext[t, pl.ds(r0 + WIDTH - j, WIDTH), ys, :])
                + (ext[t, here, pl.ds(PAD + j, ny), :] + ext[t, here, pl.ds(PAD - j, ny), :])
            )
        return core, total

    def p_chunk(k, r0, last):
        core, lap = laplace(p_ext, k + 1, r0)
        own, here = pl.ds(r0, WIDTH), pl.ds(r0 + WIDTH, WIDTH)
        grad[own] += q_ext[k + 1, here, ys, :] * lap
        if not last:
            p_ext[k + 2, here, ys, :] = (
                2.0 * core - p_ext[k, here, ys, :] + speed2[own] * lap + wavelet[0, k] * spot[own]
            )

    def result_copy(r0):
        return pltpu.make_async_copy(
            q_ext.at[STEPS + 1, pl.ds(r0 + WIDTH, WIDTH), ys],
            q_final.at[0, pl.ds(r0, WIDTH)],
            out_sem.at[r0 // WIDTH],
        )

    def q_chunk(k, r0, last):
        core, lap = laplace(q_ext, k + 1, r0)
        own, here = pl.ds(r0, WIDTH), pl.ds(r0 + WIDTH, WIDTH)
        new = 2.0 * core - q_ext[k, here, ys, :] + speed2[own] * lap + inject[k, own]
        q_ext[k + 2, here, ys, :] = new
        if last:
            result_copy(r0).start()

    chunks = (p_chunk, q_chunk)

    def step(k, last=False, after_inner=None, after_side=None):
        for f in (0, 1):
            for c in range(1, rows // WIDTH - 1):
                chunks[f](k, c * WIDTH, last)
            if f == 0 and after_inner is not None:
                after_inner()
            for side in (fast, slow):
                halo_wait(f, k, side)
                chunks[f](k, side * (rows - WIDTH), last)
                if not last:
                    halo_send(f, k + 1, side)
                elif f == 0:
                    after_side(side)

    def loop(k, carry):
        step(k)
        return carry

    lax.fori_loop(0, STEPS - 1, loop, 0)

    share = ny // shots

    def share_copy(d, part, start, length):
        target = lax.rem(shot + d, shots)
        return pltpu.make_async_remote_copy(
            src_ref=grad.at[pl.ds(start, length), pl.ds(pl.multiple_of(target * share, share), share)],
            dst_ref=others.at[d - 1, pl.ds(start, length)],
            send_sem=share_send.at[d - 1, part], recv_sem=share_recv.at[d - 1, part],
            device_id={"shot": target}, device_id_type=pl.DeviceIdType.MESH,
        )

    def inner_parts(d):
        return share_copy(d, 2, WIDTH, rows - 2 * WIDTH)

    def side_part(d, side):
        return share_copy(d, side, side * (rows - WIDTH), WIDTH)

    def send_inner():
        for d in range(1, shots):
            inner_parts(d).start()

    def send_side(side):
        for d in range(1, shots):
            side_part(d, side).start()

    step(STEPS - 1, True, send_inner, send_side)

    for d in range(1, shots):
        inner_parts(d).wait()
        for side in (fast, slow):
            side_part(d, side).wait()
    total = grad[:, pl.ds(pl.multiple_of(shot * share, share), share), :]
    for d in range(1, shots):
        total = total + others[d - 1]
    summed[...] = total * (1.0 / (STEPS * shots))
    gradient_copy = pltpu.make_async_copy(summed, gradient, load_sem.at[0])
    gradient_copy.start()

    for f in (0, 1):
        for side in (0, 1):
            @pl.when(exists(side))
            def _():
                halo_copy(f, 0, side).wait_send()

                def finish(k, carry):
                    halo_copy(f, k, side).wait_send()
                    return carry

                lax.fori_loop(1, STEPS, finish, 0)

    for c in range(rows // WIDTH):
        result_copy(c * WIDTH).wait()
    gradient_copy.wait()


def body(courant, p_current, p_later, q_current, q_later, wavelet, source_cell, receiver_cells, residual_data):
    rows, ny, nz = courant.shape
    count, shots = lax.axis_size("space"), lax.axis_size("shot")
    share = ny // shots
    hbm = pl.BlockSpec(memory_space=pltpu.HBM)
    vmem = pl.BlockSpec(memory_space=pltpu.VMEM)
    smem = pl.BlockSpec(memory_space=pltpu.SMEM)
    cells = rows * ny * nz
    call = pl.pallas_call(
        functools.partial(kernel, count, shots),
        out_shape=(
            jax.ShapeDtypeStruct((rows, share, nz), jnp.float32),
            jax.ShapeDtypeStruct((1, rows, ny, nz), jnp.float32),
        ),
        in_specs=[hbm] * 5 + [smem, smem, vmem, vmem],
        out_specs=(hbm, hbm),
        scratch_shapes=[
            pltpu.VMEM((STEPS + 1, rows + 2 * WIDTH, ny + 2 * PAD, nz), jnp.float32),
            pltpu.VMEM((STEPS + 2, rows + 2 * WIDTH, ny + 2 * PAD, nz), jnp.float32),
            pltpu.VMEM((rows, ny, nz), jnp.float32),
            pltpu.VMEM((rows, ny, nz), jnp.float32),
            pltpu.VMEM((rows, ny, nz), jnp.float32),
            pltpu.VMEM((STEPS, rows, ny, nz), jnp.float32),
            pltpu.VMEM((max(shots - 1, 1), rows, share, nz), jnp.float32),
            pltpu.VMEM((2 * nz, 2 * nz), jnp.bfloat16),
            pltpu.VMEM((rows, share, nz), jnp.float32),
            pltpu.SemaphoreType.DMA((5,)),
            pltpu.SemaphoreType.DMA((rows // WIDTH,)),
            pltpu.SemaphoreType.DMA((2, STEPS, 2)),
            pltpu.SemaphoreType.DMA((2, STEPS, 2)),
            pltpu.SemaphoreType.DMA((max(shots - 1, 1), 3)),
            pltpu.SemaphoreType.DMA((max(shots - 1, 1), 3)),
        ],
        compiler_params=pltpu.CompilerParams(
            collective_id=0, has_side_effects=True, vmem_limit_bytes=60 * 1024 * 1024
        ),
        cost_estimate=pl.CostEstimate(
            flops=2 * STEPS * 40 * cells, bytes_accessed=7 * 4 * cells, transcendentals=0
        ),
    )
    return call(
        courant, p_current, p_later, q_current, q_later, wavelet, source_cell, receiver_cells,
        jnp.swapaxes(residual_data, 0, 1),
    )


def solution(mesh):
    in_specs = (
        P("space", None, None),
        P("shot", "space", None, None),
        P("shot", "space", None, None),
        P("shot", "space", None, None),
        P("shot", "space", None, None),
        P("shot", None),
        P("shot"),
        P("shot", None),
        P("shot", None, None),
    )
    out_specs = (P("space", "shot", None), P("shot", "space", None, None))
    return jax.shard_map(body, mesh=mesh, in_specs=in_specs, out_specs=out_specs, check_vma=False)
```

```python
import functools

import jax
import jax.numpy as jnp
from jax import lax
from jax.experimental import pallas as pl
from jax.experimental.pallas import tpu as pltpu
from jax.sharding import PartitionSpec as P

STEPS = 6
WIDTH = 4
PAD = 8

coefs = (-205.0 / 72.0, 8.0 / 5.0, -1.0 / 5.0, 8.0 / 315.0, -1.0 / 560.0)


def band(depth):
    apart = jnp.abs(
        lax.broadcasted_iota(jnp.int32, (depth, depth), 0) - lax.broadcasted_iota(jnp.int32, (depth, depth), 1)
    )
    whole = jnp.zeros((depth, depth), jnp.float32)
    for j in range(1, WIDTH + 1):
        whole = jnp.where(apart == j, coefs[j], whole)
    high, low = split(whole, 2)
    return jnp.concatenate(
        [jnp.concatenate([high, low], axis=1), jnp.concatenate([high, jnp.zeros_like(high)], axis=1)], axis=0
    )


def split(value, terms):
    parts = []
    for _ in range(terms):
        part = value.astype(jnp.bfloat16)
        parts.append(part)
        value = value - part.astype(jnp.float32)
    return parts


def kernel(
    count, shots,
    courant, p_current, p_later, q_current, q_later, wavelet, source, receivers, residual,
    gradient, q_final,
    p_ext, q_ext, halos, speed2, grad, spot, inject, others, matrix, summed,
    load_sem, out_sem, send_sem, recv_sem, share_send, share_recv,
):
    rows, ny, nz = speed2.shape
    me = lax.axis_index("space")
    shot = lax.axis_index("shot")
    odd = lax.rem(me, 2)
    exts = (p_ext, q_ext)
    currents = (p_current, q_current)
    ys = pl.ds(PAD, ny)

    def neighbour(side):
        return me - 1 + 2 * side

    def exists(side):
        return jnp.logical_and(neighbour(side) >= 0, neighbour(side) < count)

    def halo_copy(f, k, side):
        if isinstance(k, int) and k == 0:
            src = currents[f].at[0, pl.ds(side * (rows - WIDTH), WIDTH)]
        else:
            src = exts[f].at[k + 1, pl.ds(WIDTH + side * (rows - WIDTH), WIDTH), ys]
        return pltpu.make_async_remote_copy(
            src_ref=src, dst_ref=halos.at[f, k, 1 - side],
            send_sem=send_sem.at[f, k, side], recv_sem=recv_sem.at[f, k, side],
            device_id={"space": neighbour(side)}, device_id_type=pl.DeviceIdType.MESH,
        )

    def halo_wait(f, k, side):
        here = halos.at[f, k, side]
        pltpu.make_async_remote_copy(
            src_ref=here, dst_ref=here,
            send_sem=send_sem.at[f, k, 1 - side], recv_sem=recv_sem.at[f, k, 1 - side],
            device_id={"space": neighbour(side)}, device_id_type=pl.DeviceIdType.MESH,
        ).wait_recv()

    slow, fast = odd, 1 - odd

    loads = [
        pltpu.make_async_copy(courant, speed2, load_sem.at[0]),
        pltpu.make_async_copy(p_current.at[0], p_ext.at[1, pl.ds(WIDTH, rows), ys], load_sem.at[1]),
        pltpu.make_async_copy(q_current.at[0], q_ext.at[1, pl.ds(WIDTH, rows), ys], load_sem.at[2]),
        pltpu.make_async_copy(p_later.at[0], p_ext.at[0, pl.ds(WIDTH, rows), ys], load_sem.at[3]),
        pltpu.make_async_copy(q_later.at[0], q_ext.at[0, pl.ds(WIDTH, rows), ys], load_sem.at[4]),
    ]
    for load in loads:
        load.start()

    barrier = pltpu.get_barrier_semaphore()
    for side in (0, 1):
        @pl.when(exists(side))
        def _():
            pl.semaphore_signal(
                barrier, inc=1, device_id={"space": neighbour(side)}, device_id_type=pl.DeviceIdType.MESH
            )
    for d in range(1, shots):
        pl.semaphore_signal(
            barrier, inc=1, device_id={"shot": lax.rem(shot + d, shots)}, device_id_type=pl.DeviceIdType.MESH
        )
    pl.semaphore_wait(
        barrier, exists(0).astype(jnp.int32) + exists(1).astype(jnp.int32) + (shots - 1)
    )
    for f in (0, 1):
        for side in (slow, fast):
            @pl.when(exists(side))
            def _():
                halo_copy(f, 0, side).start()

    matrix[...] = band(nz)
    for ext in exts:
        edge = jnp.zeros((ext.shape[0] - 1, rows, PAD, nz), jnp.float32)
        ext[1:, WIDTH:WIDTH + rows, 0:PAD, :] = edge
        ext[1:, WIDTH:WIDTH + rows, PAD + ny:PAD + ny + PAD, :] = edge
        outside = jnp.zeros((ext.shape[0] - 1, WIDTH, ny, nz), jnp.float32)
        ext[1:, 0:WIDTH, PAD:PAD + ny, :] = outside
        ext[1:, rows + WIDTH:rows + 2 * WIDTH, PAD:PAD + ny, :] = outside

    shift = nz.bit_length() - 1
    cells = receivers[...]
    cell_row = lax.shift_right_logical(cells, shift) - me * (rows * ny)
    cell_column = jnp.bitwise_and(cells, nz - 1)
    column_hit = lax.broadcasted_iota(jnp.int32, (nz, cells.shape[1]), 0) == cell_column
    values = jnp.concatenate(
        [jnp.where(column_hit, residual[k], 0.0) for k in range(STEPS)], axis=0
    )
    value_parts = split(values, 3)
    block = WIDTH * ny
    for c in range(rows // WIDTH):
        ids = lax.broadcasted_iota(jnp.int32, (block, cells.shape[1]), 0) + c * block
        row_hit = jnp.where(ids == cell_row, 1.0, 0.0).astype(jnp.bfloat16)
        total = None
        for part in value_parts:
            term = lax.dot_general(
                row_hit, part, (((1,), (1,)), ((), ())), preferred_element_type=jnp.float32
            )
            total = term if total is None else total + term
        for k in range(STEPS):
            inject[k, c * WIDTH:(c + 1) * WIDTH] = total[:, k * nz:(k + 1) * nz].reshape(WIDTH, ny, nz)
        flat = (
            (lax.broadcasted_iota(jnp.int32, (WIDTH, ny, nz), 0) + (me * rows + c * WIDTH)) * (ny * nz)
            + lax.broadcasted_iota(jnp.int32, (WIDTH, ny, nz), 1) * nz
            + lax.broadcasted_iota(jnp.int32, (WIDTH, ny, nz), 2)
        )
        spot[c * WIDTH:(c + 1) * WIDTH] = jnp.where(flat == source[0], 1.0, 0.0)
    grad[...] = jnp.zeros_like(grad)
    for load in loads:
        load.wait()
    speed2[...] = speed2[...] * speed2[...]

    def laplace(ext, t, r0):
        here = pl.ds(r0 + WIDTH, WIDTH)
        core = ext[t, here, ys, :]
        pair = jnp.concatenate(split(core, 2), axis=-1).reshape(WIDTH * ny, 2 * nz)
        along_z = jnp.dot(pair, matrix[...], preferred_element_type=jnp.float32)
        total = (along_z[:, :nz] + along_z[:, nz:]).reshape(WIDTH, ny, nz) + 3.0 * coefs[0] * core
        for j in range(1, WIDTH + 1):
            total = total + coefs[j] * (
                (ext[t, pl.ds(r0 + WIDTH + j, WIDTH), ys, :] + ext[t, pl.ds(r0 + WIDTH - j, WIDTH), ys, :])
                + (ext[t, here, pl.ds(PAD + j, ny), :] + ext[t, here, pl.ds(PAD - j, ny), :])
            )
        return core, total

    def p_chunk(k, r0, last):
        core, lap = laplace(p_ext, k + 1, r0)
        own, here = pl.ds(r0, WIDTH), pl.ds(r0 + WIDTH, WIDTH)
        grad[own] += q_ext[k + 1, here, ys, :] * lap
        if not last:
            p_ext[k + 2, here, ys, :] = (
                2.0 * core - p_ext[k, here, ys, :] + speed2[own] * lap + wavelet[0, k] * spot[own]
            )

    def q_chunk(k, r0, last):
        core, lap = laplace(q_ext, k + 1, r0)
        own, here = pl.ds(r0, WIDTH), pl.ds(r0 + WIDTH, WIDTH)
        q_ext[k + 2, here, ys, :] = 2.0 * core - q_ext[k, here, ys, :] + speed2[own] * lap + inject[k, own]

    def add_halo(f, k, side, last):
        for i in range(WIDTH):
            r = side * (rows - 1) + (1 - 2 * side) * i
            lap = None
            for j in range(i + 1, WIDTH + 1):
                away = j - i
                term = coefs[j] * halos[f, k, side, (1 - side) * (WIDTH - away) + side * (away - 1)]
                lap = term if lap is None else lap + term
            if f == 0:
                grad[r] += q_ext[k + 1, r + WIDTH, ys, :] * lap
            if f == 1 or not last:
                exts[f][k + 2, r + WIDTH, ys, :] += speed2[r] * lap

    def result_copy(part, r0, length):
        return pltpu.make_async_copy(
            q_ext.at[STEPS + 1, pl.ds(r0 + WIDTH, length), ys],
            q_final.at[0, pl.ds(r0, length)],
            out_sem.at[part],
        )

    def result_side(side):
        return result_copy(side, side * (rows - WIDTH), WIDTH)

    def result_inner():
        return result_copy(2, WIDTH, rows - 2 * WIDTH)

    chunks = (p_chunk, q_chunk)

    def step(k, last=False, after_inner=None, after_side=None):
        for f in (0, 1):
            for c in range(rows // WIDTH):
                chunks[f](k, c * WIDTH, last)
            if last:
                after_inner[f]()
            for side in (fast, slow):
                @pl.when(exists(side))
                def _():
                    halo_wait(f, k, side)
                    add_halo(f, k, side, last)
                    if not last:
                        halo_copy(f, k + 1, side).start()
                if last:
                    after_side[f](side)

    def loop(k, carry):
        step(k)
        return carry

    lax.fori_loop(0, STEPS - 1, loop, 0)

    share = ny // shots

    def share_copy(d, part, start, length):
        target = lax.rem(shot + d, shots)
        return pltpu.make_async_remote_copy(
            src_ref=grad.at[pl.ds(start, length), pl.ds(pl.multiple_of(target * share, share), share)],
            dst_ref=others.at[d - 1, pl.ds(start, length)],
            send_sem=share_send.at[d - 1, part], recv_sem=share_recv.at[d - 1, part],
            device_id={"shot": target}, device_id_type=pl.DeviceIdType.MESH,
        )

    def inner_parts(d):
        return share_copy(d, 2, WIDTH, rows - 2 * WIDTH)

    def side_part(d, side):
        return share_copy(d, side, side * (rows - WIDTH), WIDTH)

    def send_inner():
        for d in range(1, shots):
            inner_parts(d).start()

    def send_side(side):
        for d in range(1, shots):
            side_part(d, side).start()

    step(
        STEPS - 1, True,
        (send_inner, lambda: result_inner().start()),
        (send_side, lambda side: result_side(side).start()),
    )

    for d in range(1, shots):
        inner_parts(d).wait()
        for side in (fast, slow):
            side_part(d, side).wait()
    total = grad[:, pl.ds(pl.multiple_of(shot * share, share), share), :]
    for d in range(1, shots):
        total = total + others[d - 1]
    summed[...] = total * (1.0 / (STEPS * shots))
    gradient_copy = pltpu.make_async_copy(summed, gradient, load_sem.at[0])
    gradient_copy.start()

    for f in (0, 1):
        for side in (0, 1):
            @pl.when(exists(side))
            def _():
                halo_copy(f, 0, side).wait_send()

                def finish(k, carry):
                    halo_copy(f, k, side).wait_send()
                    return carry

                lax.fori_loop(1, STEPS, finish, 0)

    result_inner().wait()
    for side in (fast, slow):
        result_side(side).wait()
    gradient_copy.wait()


def copy_kernel(gradient, q_final, gradient_out, q_out, sem):
    half = q_final.shape[1] // 2
    copies = [pltpu.make_async_copy(gradient, gradient_out, sem.at[0])] + [
        pltpu.make_async_copy(q_final.at[0, pl.ds(i * half, half)], q_out.at[0, pl.ds(i * half, half)], sem.at[1 + i])
        for i in (0, 1)
    ]
    for copy in copies:
        copy.start()
    for copy in copies:
        copy.wait()


def hand_over(gradient, q_final):
    hbm = pl.BlockSpec(memory_space=pltpu.HBM)
    return pl.pallas_call(
        copy_kernel,
        out_shape=(
            jax.ShapeDtypeStruct(gradient.shape, gradient.dtype),
            jax.ShapeDtypeStruct(q_final.shape, q_final.dtype),
        ),
        in_specs=[hbm, hbm],
        out_specs=(hbm, hbm),
        scratch_shapes=[pltpu.SemaphoreType.DMA((3,))],
        compiler_params=pltpu.CompilerParams(vmem_limit_bytes=60 * 1024 * 1024),
    )(gradient, q_final)


def body(courant, p_current, p_later, q_current, q_later, wavelet, source_cell, receiver_cells, residual_data):
    rows, ny, nz = courant.shape
    count, shots = lax.axis_size("space"), lax.axis_size("shot")
    share = ny // shots
    hbm = pl.BlockSpec(memory_space=pltpu.HBM)
    vmem = pl.BlockSpec(memory_space=pltpu.VMEM)
    smem = pl.BlockSpec(memory_space=pltpu.SMEM)
    cells = rows * ny * nz
    call = pl.pallas_call(
        functools.partial(kernel, count, shots),
        out_shape=(
            jax.ShapeDtypeStruct((rows, share, nz), jnp.float32),
            jax.ShapeDtypeStruct((1, rows, ny, nz), jnp.float32),
        ),
        in_specs=[hbm] * 5 + [smem, smem, vmem, vmem],
        out_specs=(hbm, hbm),
        scratch_shapes=[
            pltpu.VMEM((STEPS + 1, rows + 2 * WIDTH, ny + 2 * PAD, nz), jnp.float32),
            pltpu.VMEM((STEPS + 2, rows + 2 * WIDTH, ny + 2 * PAD, nz), jnp.float32),
            pltpu.VMEM((2, STEPS, 2, WIDTH, ny, nz), jnp.float32),
            pltpu.VMEM((rows, ny, nz), jnp.float32),
            pltpu.VMEM((rows, ny, nz), jnp.float32),
            pltpu.VMEM((rows, ny, nz), jnp.float32),
            pltpu.VMEM((STEPS, rows, ny, nz), jnp.float32),
            pltpu.VMEM((max(shots - 1, 1), rows, share, nz), jnp.float32),
            pltpu.VMEM((2 * nz, 2 * nz), jnp.bfloat16),
            pltpu.VMEM((rows, share, nz), jnp.float32),
            pltpu.SemaphoreType.DMA((5,)),
            pltpu.SemaphoreType.DMA((3,)),
            pltpu.SemaphoreType.DMA((2, STEPS, 2)),
            pltpu.SemaphoreType.DMA((2, STEPS, 2)),
            pltpu.SemaphoreType.DMA((max(shots - 1, 1), 3)),
            pltpu.SemaphoreType.DMA((max(shots - 1, 1), 3)),
        ],
        compiler_params=pltpu.CompilerParams(
            collective_id=0, has_side_effects=True, vmem_limit_bytes=60 * 1024 * 1024
        ),
        cost_estimate=pl.CostEstimate(
            flops=2 * STEPS * 40 * cells, bytes_accessed=7 * 4 * cells, transcendentals=0
        ),
    )
    gradient, q_final = call(
        courant, p_current, p_later, q_current, q_later, wavelet, source_cell, receiver_cells,
        jnp.swapaxes(residual_data, 0, 1),
    )
    return hand_over(gradient, q_final)


def solution(mesh):
    in_specs = (
        P("space", None, None),
        P("shot", "space", None, None),
        P("shot", "space", None, None),
        P("shot", "space", None, None),
        P("shot", "space", None, None),
        P("shot", None),
        P("shot"),
        P("shot", None),
        P("shot", None, None),
    )
    out_specs = (P("space", "shot", None), P("shot", "space", None, None))
    return jax.shard_map(body, mesh=mesh, in_specs=in_specs, out_specs=out_specs, check_vma=False)
```

```python
import functools

import jax
import jax.numpy as jnp
from jax import lax
from jax.experimental import pallas as pl
from jax.experimental.pallas import tpu as pltpu
from jax.sharding import PartitionSpec as P

STEPS = 6
WIDTH = 4
PAD = 8

coefs = (-205.0 / 72.0, 8.0 / 5.0, -1.0 / 5.0, 8.0 / 315.0, -1.0 / 560.0)


def band(depth):
    apart = jnp.abs(
        lax.broadcasted_iota(jnp.int32, (depth, depth), 0) - lax.broadcasted_iota(jnp.int32, (depth, depth), 1)
    )
    whole = jnp.zeros((depth, depth), jnp.float32)
    for j in range(1, WIDTH + 1):
        whole = jnp.where(apart == j, coefs[j], whole)
    high, low = split(whole, 2)
    return jnp.concatenate(
        [jnp.concatenate([high, low], axis=1), jnp.concatenate([high, jnp.zeros_like(high)], axis=1)], axis=0
    )


def split(value, terms):
    parts = []
    for _ in range(terms):
        part = value.astype(jnp.bfloat16)
        parts.append(part)
        value = value - part.astype(jnp.float32)
    return parts


def kernel(
    count, shots,
    courant, p_current, p_later, q_current, q_later, wavelet, source, receivers, residual,
    gradient, q_final,
    p_ext, q_ext, halos, speed2, grad, spot, inject, others, matrix, summed,
    load_sem, out_sem, send_sem, recv_sem, share_send, share_recv,
):
    rows, ny, nz = speed2.shape
    me = lax.axis_index("space")
    shot = lax.axis_index("shot")
    odd = lax.rem(me, 2)
    exts = (p_ext, q_ext)
    currents = (p_current, q_current)
    ys = pl.ds(PAD, ny)

    def neighbour(side):
        return me - 1 + 2 * side

    def exists(side):
        return jnp.logical_and(neighbour(side) >= 0, neighbour(side) < count)

    def halo_copy(f, k, side):
        if isinstance(k, int) and k == 0:
            src = currents[f].at[0, pl.ds(side * (rows - WIDTH), WIDTH)]
        else:
            src = exts[f].at[k + 1, pl.ds(WIDTH + side * (rows - WIDTH), WIDTH), ys]
        return pltpu.make_async_remote_copy(
            src_ref=src, dst_ref=halos.at[f, k, 1 - side],
            send_sem=send_sem.at[f, k, side], recv_sem=recv_sem.at[f, k, side],
            device_id={"space": neighbour(side)}, device_id_type=pl.DeviceIdType.MESH,
        )

    def halo_wait(f, k, side):
        here = halos.at[f, k, side]
        pltpu.make_async_remote_copy(
            src_ref=here, dst_ref=here,
            send_sem=send_sem.at[f, k, 1 - side], recv_sem=recv_sem.at[f, k, 1 - side],
            device_id={"space": neighbour(side)}, device_id_type=pl.DeviceIdType.MESH,
        ).wait_recv()

    slow, fast = odd, 1 - odd

    loads = [
        pltpu.make_async_copy(courant, speed2, load_sem.at[0]),
        pltpu.make_async_copy(p_current.at[0], p_ext.at[1, pl.ds(WIDTH, rows), ys], load_sem.at[1]),
        pltpu.make_async_copy(q_current.at[0], q_ext.at[1, pl.ds(WIDTH, rows), ys], load_sem.at[2]),
        pltpu.make_async_copy(p_later.at[0], p_ext.at[0, pl.ds(WIDTH, rows), ys], load_sem.at[3]),
        pltpu.make_async_copy(q_later.at[0], q_ext.at[0, pl.ds(WIDTH, rows), ys], load_sem.at[4]),
    ]
    for load in loads:
        load.start()

    barrier = pltpu.get_barrier_semaphore()
    for side in (0, 1):
        @pl.when(exists(side))
        def _():
            pl.semaphore_signal(
                barrier, inc=1, device_id={"space": neighbour(side)}, device_id_type=pl.DeviceIdType.MESH
            )
    for d in range(1, shots):
        pl.semaphore_signal(
            barrier, inc=1, device_id={"shot": lax.rem(shot + d, shots)}, device_id_type=pl.DeviceIdType.MESH
        )
    pl.semaphore_wait(
        barrier, exists(0).astype(jnp.int32) + exists(1).astype(jnp.int32) + (shots - 1)
    )
    for f in (0, 1):
        for side in (slow, fast):
            @pl.when(exists(side))
            def _():
                halo_copy(f, 0, side).start()

    matrix[...] = band(nz)
    for ext in exts:
        edge = jnp.zeros((ext.shape[0] - 1, rows, PAD, nz), jnp.float32)
        ext[1:, WIDTH:WIDTH + rows, 0:PAD, :] = edge
        ext[1:, WIDTH:WIDTH + rows, PAD + ny:PAD + ny + PAD, :] = edge
        outside = jnp.zeros((ext.shape[0] - 1, WIDTH, ny, nz), jnp.float32)
        ext[1:, 0:WIDTH, PAD:PAD + ny, :] = outside
        ext[1:, rows + WIDTH:rows + 2 * WIDTH, PAD:PAD + ny, :] = outside

    for c in range(rows // WIDTH):
        flat = (
            (lax.broadcasted_iota(jnp.int32, (WIDTH, ny, nz), 0) + (me * rows + c * WIDTH)) * (ny * nz)
            + lax.broadcasted_iota(jnp.int32, (WIDTH, ny, nz), 1) * nz
            + lax.broadcasted_iota(jnp.int32, (WIDTH, ny, nz), 2)
        )
        spot[c * WIDTH:(c + 1) * WIDTH] = jnp.where(flat == source[0], 1.0, 0.0)
    grad[...] = jnp.zeros_like(grad)
    for load in (loads[0], loads[1], loads[2], loads[3]):
        load.wait()
    speed2[...] = speed2[...] * speed2[...]

    def prepare_injection():
        shift = nz.bit_length() - 1
        cells = receivers[...]
        cell_row = lax.shift_right_logical(cells, shift) - me * (rows * ny)
        cell_column = jnp.bitwise_and(cells, nz - 1)
        column_hit = lax.broadcasted_iota(jnp.int32, (nz, cells.shape[1]), 0) == cell_column
        values = jnp.concatenate(
            [jnp.where(column_hit, residual[k], 0.0) for k in range(STEPS)], axis=0
        )
        value_parts = split(values, 3)
        block = WIDTH * ny
        for c in range(rows // WIDTH):
            ids = lax.broadcasted_iota(jnp.int32, (block, cells.shape[1]), 0) + c * block
            row_hit = jnp.where(ids == cell_row, 1.0, 0.0).astype(jnp.bfloat16)
            total = None
            for part in value_parts:
                term = lax.dot_general(
                    row_hit, part, (((1,), (1,)), ((), ())), preferred_element_type=jnp.float32
                )
                total = term if total is None else total + term
            for k in range(STEPS):
                inject[k, c * WIDTH:(c + 1) * WIDTH] = total[:, k * nz:(k + 1) * nz].reshape(WIDTH, ny, nz)

    def laplace(ext, t, r0):
        here = pl.ds(r0 + WIDTH, WIDTH)
        core = ext[t, here, ys, :]
        pair = jnp.concatenate(split(core, 2), axis=-1).reshape(WIDTH * ny, 2 * nz)
        along_z = jnp.dot(pair, matrix[...], preferred_element_type=jnp.float32)
        total = (along_z[:, :nz] + along_z[:, nz:]).reshape(WIDTH, ny, nz) + 3.0 * coefs[0] * core
        for j in range(1, WIDTH + 1):
            total = total + coefs[j] * (
                (ext[t, pl.ds(r0 + WIDTH + j, WIDTH), ys, :] + ext[t, pl.ds(r0 + WIDTH - j, WIDTH), ys, :])
                + (ext[t, here, pl.ds(PAD + j, ny), :] + ext[t, here, pl.ds(PAD - j, ny), :])
            )
        return core, total

    def p_chunk(k, r0, last):
        core, lap = laplace(p_ext, k + 1, r0)
        own, here = pl.ds(r0, WIDTH), pl.ds(r0 + WIDTH, WIDTH)
        grad[own] += q_ext[k + 1, here, ys, :] * lap
        if not last:
            p_ext[k + 2, here, ys, :] = (
                2.0 * core - p_ext[k, here, ys, :] + speed2[own] * lap + wavelet[0, k] * spot[own]
            )

    def q_chunk(k, r0, last):
        core, lap = laplace(q_ext, k + 1, r0)
        own, here = pl.ds(r0, WIDTH), pl.ds(r0 + WIDTH, WIDTH)
        q_ext[k + 2, here, ys, :] = 2.0 * core - q_ext[k, here, ys, :] + speed2[own] * lap + inject[k, own]

    def add_halo(f, k, side, last):
        for i in range(WIDTH):
            r = side * (rows - 1) + (1 - 2 * side) * i
            lap = None
            for j in range(i + 1, WIDTH + 1):
                away = j - i
                term = coefs[j] * halos[f, k, side, (1 - side) * (WIDTH - away) + side * (away - 1)]
                lap = term if lap is None else lap + term
            if f == 0:
                grad[r] += q_ext[k + 1, r + WIDTH, ys, :] * lap
            if f == 1 or not last:
                exts[f][k + 2, r + WIDTH, ys, :] += speed2[r] * lap

    def result_copy(part, r0, length):
        return pltpu.make_async_copy(
            q_ext.at[STEPS + 1, pl.ds(r0 + WIDTH, length), ys],
            q_final.at[0, pl.ds(r0, length)],
            out_sem.at[part],
        )

    def result_side(side):
        return result_copy(side, side * (rows - WIDTH), WIDTH)

    def result_inner():
        return result_copy(2, WIDTH, rows - 2 * WIDTH)

    chunks = (p_chunk, q_chunk)

    def step(k, last=False, after_inner=None, after_side=None):
        for f in (0, 1):
            if f == 1 and isinstance(k, int) and k == 0:
                prepare_injection()
                loads[4].wait()
            for c in range(rows // WIDTH):
                chunks[f](k, c * WIDTH, last)
            if last:
                after_inner[f]()
            for side in (fast, slow):
                @pl.when(exists(side))
                def _():
                    halo_wait(f, k, side)
                    add_halo(f, k, side, last)
                    if not last:
                        halo_copy(f, k + 1, side).start()
                if last:
                    after_side[f](side)

    def loop(k, carry):
        step(k)
        return carry

    step(0)
    lax.fori_loop(1, STEPS - 1, loop, 0)

    share = ny // shots

    def share_copy(d, part, start, length):
        target = lax.rem(shot + d, shots)
        return pltpu.make_async_remote_copy(
            src_ref=grad.at[pl.ds(start, length), pl.ds(pl.multiple_of(target * share, share), share)],
            dst_ref=others.at[d - 1, pl.ds(start, length)],
            send_sem=share_send.at[d - 1, part], recv_sem=share_recv.at[d - 1, part],
            device_id={"shot": target}, device_id_type=pl.DeviceIdType.MESH,
        )

    def inner_parts(d):
        return share_copy(d, 2, WIDTH, rows - 2 * WIDTH)

    def side_part(d, side):
        return share_copy(d, side, side * (rows - WIDTH), WIDTH)

    def send_inner():
        for d in range(1, shots):
            inner_parts(d).start()

    def send_side(side):
        for d in range(1, shots):
            side_part(d, side).start()

    step(
        STEPS - 1, True,
        (send_inner, lambda: result_inner().start()),
        (send_side, lambda side: result_side(side).start()),
    )

    for d in range(1, shots):
        inner_parts(d).wait()
        for side in (fast, slow):
            side_part(d, side).wait()
    total = grad[:, pl.ds(pl.multiple_of(shot * share, share), share), :]
    for d in range(1, shots):
        total = total + others[d - 1]
    summed[...] = total * (1.0 / (STEPS * shots))
    gradient_copy = pltpu.make_async_copy(summed, gradient, load_sem.at[0])
    gradient_copy.start()

    for f in (0, 1):
        for side in (0, 1):
            @pl.when(exists(side))
            def _():
                halo_copy(f, 0, side).wait_send()

                def finish(k, carry):
                    halo_copy(f, k, side).wait_send()
                    return carry

                lax.fori_loop(1, STEPS, finish, 0)

    result_inner().wait()
    for side in (fast, slow):
        result_side(side).wait()
    gradient_copy.wait()


def body(courant, p_current, p_later, q_current, q_later, wavelet, source_cell, receiver_cells, residual_data):
    rows, ny, nz = courant.shape
    count, shots = lax.axis_size("space"), lax.axis_size("shot")
    share = ny // shots
    hbm = pl.BlockSpec(memory_space=pltpu.HBM)
    vmem = pl.BlockSpec(memory_space=pltpu.VMEM)
    smem = pl.BlockSpec(memory_space=pltpu.SMEM)
    cells = rows * ny * nz
    call = pl.pallas_call(
        functools.partial(kernel, count, shots),
        out_shape=(
            jax.ShapeDtypeStruct((rows, share, nz), jnp.float32),
            jax.ShapeDtypeStruct((1, rows, ny, nz), jnp.float32),
        ),
        in_specs=[hbm] * 5 + [smem, smem, vmem, vmem],
        out_specs=(hbm, hbm),
        scratch_shapes=[
            pltpu.VMEM((STEPS + 1, rows + 2 * WIDTH, ny + 2 * PAD, nz), jnp.float32),
            pltpu.VMEM((STEPS + 2, rows + 2 * WIDTH, ny + 2 * PAD, nz), jnp.float32),
            pltpu.VMEM((2, STEPS, 2, WIDTH, ny, nz), jnp.float32),
            pltpu.VMEM((rows, ny, nz), jnp.float32),
            pltpu.VMEM((rows, ny, nz), jnp.float32),
            pltpu.VMEM((rows, ny, nz), jnp.float32),
            pltpu.VMEM((STEPS, rows, ny, nz), jnp.float32),
            pltpu.VMEM((max(shots - 1, 1), rows, share, nz), jnp.float32),
            pltpu.VMEM((2 * nz, 2 * nz), jnp.bfloat16),
            pltpu.VMEM((rows, share, nz), jnp.float32),
            pltpu.SemaphoreType.DMA((5,)),
            pltpu.SemaphoreType.DMA((3,)),
            pltpu.SemaphoreType.DMA((2, STEPS, 2)),
            pltpu.SemaphoreType.DMA((2, STEPS, 2)),
            pltpu.SemaphoreType.DMA((max(shots - 1, 1), 3)),
            pltpu.SemaphoreType.DMA((max(shots - 1, 1), 3)),
        ],
        compiler_params=pltpu.CompilerParams(
            collective_id=0, has_side_effects=True, vmem_limit_bytes=60 * 1024 * 1024
        ),
        cost_estimate=pl.CostEstimate(
            flops=2 * STEPS * 40 * cells, bytes_accessed=7 * 4 * cells, transcendentals=0
        ),
    )
    return call(
        courant, p_current, p_later, q_current, q_later, wavelet, source_cell, receiver_cells,
        jnp.swapaxes(residual_data, 0, 1),
    )


def solution(mesh):
    in_specs = (
        P("space", None, None),
        P("shot", "space", None, None),
        P("shot", "space", None, None),
        P("shot", "space", None, None),
        P("shot", "space", None, None),
        P("shot", None),
        P("shot"),
        P("shot", None),
        P("shot", None, None),
    )
    out_specs = (P("space", "shot", None), P("shot", "space", None, None))
    return jax.shard_map(body, mesh=mesh, in_specs=in_specs, out_specs=out_specs, check_vma=False)
```

```python
import functools

import jax
import jax.numpy as jnp
from jax import lax
from jax.experimental import pallas as pl
from jax.experimental.pallas import tpu as pltpu
from jax.sharding import PartitionSpec as P

STEPS = 6
WIDTH = 4
PAD = 8

coefs = (-205.0 / 72.0, 8.0 / 5.0, -1.0 / 5.0, 8.0 / 315.0, -1.0 / 560.0)


def band(depth):
    apart = jnp.abs(
        lax.broadcasted_iota(jnp.int32, (depth, depth), 0) - lax.broadcasted_iota(jnp.int32, (depth, depth), 1)
    )
    whole = jnp.zeros((depth, depth), jnp.float32)
    for j in range(1, WIDTH + 1):
        whole = jnp.where(apart == j, coefs[j], whole)
    high, low = split(whole, 2)
    return jnp.concatenate(
        [jnp.concatenate([high, low], axis=1), jnp.concatenate([high, jnp.zeros_like(high)], axis=1)], axis=0
    )


def split(value, terms):
    parts = []
    for _ in range(terms):
        part = value.astype(jnp.bfloat16)
        parts.append(part)
        value = value - part.astype(jnp.float32)
    return parts


def kernel(
    count, shots,
    courant, p_current, p_later, q_current, q_later, wavelet, source, receivers, residual,
    gradient, q_final,
    p_ext, q_ext, halos, passing, speed2, grad, spot, inject, others, matrix, summed,
    load_sem, out_sem, send_sem, recv_sem, share_send, share_recv,
    row_send, row_recv, pass_send, pass_recv,
):
    rows, ny, nz = speed2.shape
    me = lax.axis_index("space")
    shot = lax.axis_index("shot")
    odd = lax.rem(me, 2)
    exts = (p_ext, q_ext)
    currents = (p_current, q_current)
    ys = pl.ds(PAD, ny)

    def neighbour(side):
        return me - 1 + 2 * side

    def exists(side):
        return jnp.logical_and(neighbour(side) >= 0, neighbour(side) < count)

    def halo_copy(f, k, side):
        if isinstance(k, int) and k == 0:
            src = currents[f].at[0, pl.ds(side * (rows - WIDTH), WIDTH)]
        else:
            src = exts[f].at[k + 1, pl.ds(WIDTH + side * (rows - WIDTH), WIDTH), ys]
        return pltpu.make_async_remote_copy(
            src_ref=src, dst_ref=halos.at[f, k, 1 - side],
            send_sem=send_sem.at[f, k, side], recv_sem=recv_sem.at[f, k, side],
            device_id={"space": neighbour(side)}, device_id_type=pl.DeviceIdType.MESH,
        )

    def halo_wait(f, k, side):
        here = halos.at[f, k, side]
        pltpu.make_async_remote_copy(
            src_ref=here, dst_ref=here,
            send_sem=send_sem.at[f, k, 1 - side], recv_sem=recv_sem.at[f, k, 1 - side],
            device_id={"space": neighbour(side)}, device_id_type=pl.DeviceIdType.MESH,
        ).wait_recv()

    slow, fast = odd, 1 - odd

    level, levels = me // 4, count // 4
    place = lax.rem(me, 4)
    apart = jnp.logical_or(place == 0, place == 3)
    ahead = 2 * odd - 1
    by_way = odd * ((WIDTH * (level + 1)) // levels) + (1 - odd) * ((WIDTH * (levels - level)) // levels)
    passed = odd * ((WIDTH * level) // levels) + (1 - odd) * ((WIDTH * (levels - 1 - level)) // levels)
    behind = me - 4 * ahead
    passes = jnp.logical_and(apart, jnp.logical_and(behind >= 0, behind < count))

    def row_copy(f, k, i, around):
        if isinstance(k, int) and k == 0:
            src = currents[f].at[0, slow * (rows - WIDTH) + i]
        else:
            src = exts[f].at[k + 1, WIDTH + slow * (rows - WIDTH) + i, ys]
        return pltpu.make_async_remote_copy(
            src_ref=src, dst_ref=passing.at[f, k, i] if around else halos.at[f, k, 1 - slow, i],
            send_sem=row_send.at[f, k, i], recv_sem=(pass_recv if around else row_recv).at[f, k, i],
            device_id={"space": me + (4 if around else 1) * ahead}, device_id_type=pl.DeviceIdType.MESH,
        )

    def pass_copy(f, k, i):
        return pltpu.make_async_remote_copy(
            src_ref=passing.at[f, k, i], dst_ref=halos.at[f, k, 1 - slow, i],
            send_sem=pass_send.at[f, k, i], recv_sem=row_recv.at[f, k, i],
            device_id={"space": me - 3 * ahead}, device_id_type=pl.DeviceIdType.MESH,
        )

    def pass_on(f, k):
        for i in range(WIDTH):
            @pl.when(jnp.logical_and(passes, i < passed))
            def _():
                pltpu.make_async_remote_copy(
                    src_ref=passing.at[f, k, i], dst_ref=passing.at[f, k, i],
                    send_sem=row_send.at[f, k, i], recv_sem=pass_recv.at[f, k, i],
                    device_id={"space": behind}, device_id_type=pl.DeviceIdType.MESH,
                ).wait_recv()
                pass_copy(f, k, i).start()

    def send(f, k, by_rows, side):
        if by_rows:
            for i in range(WIDTH):
                @pl.when(i < by_way)
                def _():
                    row_copy(f, k, i, True).start()

                @pl.when(i >= by_way)
                def _():
                    row_copy(f, k, i, False).start()
        else:
            halo_copy(f, k, side).start()

    def arrive(f, k, by_rows, side):
        if by_rows:
            for i in range(WIDTH):
                here = halos.at[f, k, slow, i]
                pltpu.make_async_remote_copy(
                    src_ref=here, dst_ref=here, send_sem=row_send.at[f, k, i], recv_sem=row_recv.at[f, k, i],
                    device_id={"space": me + ahead}, device_id_type=pl.DeviceIdType.MESH,
                ).wait_recv()
        else:
            halo_wait(f, k, side)

    def either(side, work):
        if side is fast:
            pl.when(exists(side))(lambda: work(False))
        else:
            pl.when(jnp.logical_and(exists(side), apart))(lambda: work(True))
            pl.when(jnp.logical_and(exists(side), jnp.logical_not(apart)))(lambda: work(False))

    loads = [
        pltpu.make_async_copy(courant, speed2, load_sem.at[0]),
        pltpu.make_async_copy(p_current.at[0], p_ext.at[1, pl.ds(WIDTH, rows), ys], load_sem.at[1]),
        pltpu.make_async_copy(q_current.at[0], q_ext.at[1, pl.ds(WIDTH, rows), ys], load_sem.at[2]),
        pltpu.make_async_copy(p_later.at[0], p_ext.at[0, pl.ds(WIDTH, rows), ys], load_sem.at[3]),
        pltpu.make_async_copy(q_later.at[0], q_ext.at[0, pl.ds(WIDTH, rows), ys], load_sem.at[4]),
    ]
    for load in loads:
        load.start()

    barrier = pltpu.get_barrier_semaphore()
    for side in (0, 1):
        @pl.when(exists(side))
        def _():
            pl.semaphore_signal(
                barrier, inc=1, device_id={"space": neighbour(side)}, device_id_type=pl.DeviceIdType.MESH
            )
    meet = [(apart, me - 3 * ahead)]
    for way in (-4, 4):
        meet.append((jnp.logical_and(apart, jnp.logical_and(me + way >= 0, me + way < count)), me + way))
    for wanted, other in meet:
        @pl.when(wanted)
        def _():
            pl.semaphore_signal(
                barrier, inc=1, device_id={"space": other}, device_id_type=pl.DeviceIdType.MESH
            )
    for d in range(1, shots):
        pl.semaphore_signal(
            barrier, inc=1, device_id={"shot": lax.rem(shot + d, shots)}, device_id_type=pl.DeviceIdType.MESH
        )
    pl.semaphore_wait(
        barrier, exists(0).astype(jnp.int32) + exists(1).astype(jnp.int32) + (shots - 1)
        + sum(wanted.astype(jnp.int32) for wanted, _ in meet)
    )
    for f in (0, 1):
        for side in (slow, fast):
            either(side, lambda by_rows: send(f, 0, by_rows, side))

    matrix[...] = band(nz)
    for ext in exts:
        edge = jnp.zeros((ext.shape[0] - 1, rows, PAD, nz), jnp.float32)
        ext[1:, WIDTH:WIDTH + rows, 0:PAD, :] = edge
        ext[1:, WIDTH:WIDTH + rows, PAD + ny:PAD + ny + PAD, :] = edge
        outside = jnp.zeros((ext.shape[0] - 1, WIDTH, ny, nz), jnp.float32)
        ext[1:, 0:WIDTH, PAD:PAD + ny, :] = outside
        ext[1:, rows + WIDTH:rows + 2 * WIDTH, PAD:PAD + ny, :] = outside

    for c in range(rows // WIDTH):
        flat = (
            (lax.broadcasted_iota(jnp.int32, (WIDTH, ny, nz), 0) + (me * rows + c * WIDTH)) * (ny * nz)
            + lax.broadcasted_iota(jnp.int32, (WIDTH, ny, nz), 1) * nz
            + lax.broadcasted_iota(jnp.int32, (WIDTH, ny, nz), 2)
        )
        spot[c * WIDTH:(c + 1) * WIDTH] = jnp.where(flat == source[0], 1.0, 0.0)
    grad[...] = jnp.zeros_like(grad)
    for load in (loads[0], loads[1], loads[2], loads[3]):
        load.wait()
    speed2[...] = speed2[...] * speed2[...]

    def prepare_injection():
        shift = nz.bit_length() - 1
        cells = receivers[...]
        cell_row = lax.shift_right_logical(cells, shift) - me * (rows * ny)
        cell_column = jnp.bitwise_and(cells, nz - 1)
        column_hit = lax.broadcasted_iota(jnp.int32, (nz, cells.shape[1]), 0) == cell_column
        values = jnp.concatenate(
            [jnp.where(column_hit, residual[k], 0.0) for k in range(STEPS)], axis=0
        )
        value_parts = split(values, 3)
        block = WIDTH * ny
        for c in range(rows // WIDTH):
            ids = lax.broadcasted_iota(jnp.int32, (block, cells.shape[1]), 0) + c * block
            row_hit = jnp.where(ids == cell_row, 1.0, 0.0).astype(jnp.bfloat16)
            total = None
            for part in value_parts:
                term = lax.dot_general(
                    row_hit, part, (((1,), (1,)), ((), ())), preferred_element_type=jnp.float32
                )
                total = term if total is None else total + term
            for k in range(STEPS):
                inject[k, c * WIDTH:(c + 1) * WIDTH] = total[:, k * nz:(k + 1) * nz].reshape(WIDTH, ny, nz)

    def laplace(ext, t, r0):
        here = pl.ds(r0 + WIDTH, WIDTH)
        core = ext[t, here, ys, :]
        pair = jnp.concatenate(split(core, 2), axis=-1).reshape(WIDTH * ny, 2 * nz)
        along_z = jnp.dot(pair, matrix[...], preferred_element_type=jnp.float32)
        total = (along_z[:, :nz] + along_z[:, nz:]).reshape(WIDTH, ny, nz) + 3.0 * coefs[0] * core
        for j in range(1, WIDTH + 1):
            total = total + coefs[j] * (
                (ext[t, pl.ds(r0 + WIDTH + j, WIDTH), ys, :] + ext[t, pl.ds(r0 + WIDTH - j, WIDTH), ys, :])
                + (ext[t, here, pl.ds(PAD + j, ny), :] + ext[t, here, pl.ds(PAD - j, ny), :])
            )
        return core, total

    def p_chunk(k, r0, last):
        core, lap = laplace(p_ext, k + 1, r0)
        own, here = pl.ds(r0, WIDTH), pl.ds(r0 + WIDTH, WIDTH)
        grad[own] += q_ext[k + 1, here, ys, :] * lap
        if not last:
            p_ext[k + 2, here, ys, :] = (
                2.0 * core - p_ext[k, here, ys, :] + speed2[own] * lap + wavelet[0, k] * spot[own]
            )

    def q_chunk(k, r0, last):
        core, lap = laplace(q_ext, k + 1, r0)
        own, here = pl.ds(r0, WIDTH), pl.ds(r0 + WIDTH, WIDTH)
        q_ext[k + 2, here, ys, :] = 2.0 * core - q_ext[k, here, ys, :] + speed2[own] * lap + inject[k, own]

    def add_halo(f, k, side, last):
        for i in range(WIDTH):
            r = side * (rows - 1) + (1 - 2 * side) * i
            lap = None
            for j in range(i + 1, WIDTH + 1):
                away = j - i
                term = coefs[j] * halos[f, k, side, (1 - side) * (WIDTH - away) + side * (away - 1)]
                lap = term if lap is None else lap + term
            if f == 0:
                grad[r] += q_ext[k + 1, r + WIDTH, ys, :] * lap
            if f == 1 or not last:
                exts[f][k + 2, r + WIDTH, ys, :] += speed2[r] * lap

    def result_copy(part, r0, length):
        return pltpu.make_async_copy(
            q_ext.at[STEPS + 1, pl.ds(r0 + WIDTH, length), ys],
            q_final.at[0, pl.ds(r0, length)],
            out_sem.at[part],
        )

    def result_side(side):
        return result_copy(side, side * (rows - WIDTH), WIDTH)

    def result_inner():
        return result_copy(2, WIDTH, rows - 2 * WIDTH)

    chunks = (p_chunk, q_chunk)

    def step(k, last=False, after_inner=None, after_side=None):
        for f in (0, 1):
            if f == 1 and isinstance(k, int) and k == 0:
                prepare_injection()
                loads[4].wait()
            for c in range(rows // WIDTH):
                chunks[f](k, c * WIDTH, last)
            if last:
                after_inner[f]()
            if f == 0:
                pass_on(1, k)
            elif not last:
                pass_on(0, k + 1)
            for side in (fast, slow):
                either(side, lambda by_rows: arrive(f, k, by_rows, side))

                @pl.when(exists(side))
                def _():
                    add_halo(f, k, side, last)

                if not last:
                    either(side, lambda by_rows: send(f, k + 1, by_rows, side))
                if last:
                    after_side[f](side)

    def loop(k, carry):
        step(k)
        return carry

    pass_on(0, 0)
    step(0)
    lax.fori_loop(1, STEPS - 1, loop, 0)

    share = ny // shots

    def share_copy(d, part, start, length):
        target = lax.rem(shot + d, shots)
        return pltpu.make_async_remote_copy(
            src_ref=grad.at[pl.ds(start, length), pl.ds(pl.multiple_of(target * share, share), share)],
            dst_ref=others.at[d - 1, pl.ds(start, length)],
            send_sem=share_send.at[d - 1, part], recv_sem=share_recv.at[d - 1, part],
            device_id={"shot": target}, device_id_type=pl.DeviceIdType.MESH,
        )

    def inner_parts(d):
        return share_copy(d, 2, WIDTH, rows - 2 * WIDTH)

    def side_part(d, side):
        return share_copy(d, side, side * (rows - WIDTH), WIDTH)

    def send_inner():
        for d in range(1, shots):
            inner_parts(d).start()

    def send_side(side):
        for d in range(1, shots):
            side_part(d, side).start()

    step(
        STEPS - 1, True,
        (send_inner, lambda: result_inner().start()),
        (send_side, lambda side: result_side(side).start()),
    )

    for d in range(1, shots):
        inner_parts(d).wait()
        for side in (fast, slow):
            side_part(d, side).wait()
    total = grad[:, pl.ds(pl.multiple_of(shot * share, share), share), :]
    for d in range(1, shots):
        total = total + others[d - 1]
    summed[...] = total * (1.0 / (STEPS * shots))
    gradient_copy = pltpu.make_async_copy(summed, gradient, load_sem.at[0])
    gradient_copy.start()

    def sent(f, k, by_rows, side):
        if by_rows:
            for i in range(WIDTH):
                row_copy(f, k, i, False).wait_send()
        else:
            halo_copy(f, k, side).wait_send()

    def finish(k, carry=0):
        for f in (0, 1):
            for side in (fast, slow):
                either(side, lambda by_rows: sent(f, k, by_rows, side))
            for i in range(WIDTH):
                @pl.when(jnp.logical_and(passes, i < passed))
                def _():
                    pass_copy(f, k, i).wait_send()
        return carry

    finish(0)
    lax.fori_loop(1, STEPS, finish, 0)
    result_inner().wait()
    for side in (fast, slow):
        result_side(side).wait()
    gradient_copy.wait()


def body(courant, p_current, p_later, q_current, q_later, wavelet, source_cell, receiver_cells, residual_data):
    rows, ny, nz = courant.shape
    count, shots = lax.axis_size("space"), lax.axis_size("shot")
    share = ny // shots
    hbm = pl.BlockSpec(memory_space=pltpu.HBM)
    vmem = pl.BlockSpec(memory_space=pltpu.VMEM)
    smem = pl.BlockSpec(memory_space=pltpu.SMEM)
    cells = rows * ny * nz
    call = pl.pallas_call(
        functools.partial(kernel, count, shots),
        out_shape=(
            jax.ShapeDtypeStruct((rows, share, nz), jnp.float32),
            jax.ShapeDtypeStruct((1, rows, ny, nz), jnp.float32),
        ),
        in_specs=[hbm] * 5 + [smem, smem, vmem, vmem],
        out_specs=(hbm, hbm),
        scratch_shapes=[
            pltpu.VMEM((STEPS + 1, rows + 2 * WIDTH, ny + 2 * PAD, nz), jnp.float32),
            pltpu.VMEM((STEPS + 2, rows + 2 * WIDTH, ny + 2 * PAD, nz), jnp.float32),
            pltpu.VMEM((2, STEPS, 2, WIDTH, ny, nz), jnp.float32),
            pltpu.VMEM((2, STEPS, WIDTH, ny, nz), jnp.float32),
            pltpu.VMEM((rows, ny, nz), jnp.float32),
            pltpu.VMEM((rows, ny, nz), jnp.float32),
            pltpu.VMEM((rows, ny, nz), jnp.float32),
            pltpu.VMEM((STEPS, rows, ny, nz), jnp.float32),
            pltpu.VMEM((max(shots - 1, 1), rows, share, nz), jnp.float32),
            pltpu.VMEM((2 * nz, 2 * nz), jnp.bfloat16),
            pltpu.VMEM((rows, share, nz), jnp.float32),
            pltpu.SemaphoreType.DMA((5,)),
            pltpu.SemaphoreType.DMA((3,)),
            pltpu.SemaphoreType.DMA((2, STEPS, 2)),
            pltpu.SemaphoreType.DMA((2, STEPS, 2)),
            pltpu.SemaphoreType.DMA((max(shots - 1, 1), 3)),
            pltpu.SemaphoreType.DMA((max(shots - 1, 1), 3)),
            pltpu.SemaphoreType.DMA((2, STEPS, WIDTH)),
            pltpu.SemaphoreType.DMA((2, STEPS, WIDTH)),
            pltpu.SemaphoreType.DMA((2, STEPS, WIDTH)),
            pltpu.SemaphoreType.DMA((2, STEPS, WIDTH)),
        ],
        compiler_params=pltpu.CompilerParams(
            collective_id=0, has_side_effects=True, vmem_limit_bytes=60 * 1024 * 1024
        ),
        cost_estimate=pl.CostEstimate(
            flops=2 * STEPS * 40 * cells, bytes_accessed=7 * 4 * cells, transcendentals=0
        ),
    )
    return call(
        courant, p_current, p_later, q_current, q_later, wavelet, source_cell, receiver_cells,
        jnp.swapaxes(residual_data, 0, 1),
    )


def solution(mesh):
    in_specs = (
        P("space", None, None),
        P("shot", "space", None, None),
        P("shot", "space", None, None),
        P("shot", "space", None, None),
        P("shot", "space", None, None),
        P("shot", None),
        P("shot"),
        P("shot", None),
        P("shot", None, None),
    )
    out_specs = (P("space", "shot", None), P("shot", "space", None, None))
    return jax.shard_map(body, mesh=mesh, in_specs=in_specs, out_specs=out_specs, check_vma=False)
```

```python
import functools

import jax
import jax.numpy as jnp
from jax import lax
from jax.experimental import pallas as pl
from jax.experimental.pallas import tpu as pltpu
from jax.sharding import PartitionSpec as P

STEPS = 6
WIDTH = 4
PAD = 8

coefs = (-205.0 / 72.0, 8.0 / 5.0, -1.0 / 5.0, 8.0 / 315.0, -1.0 / 560.0)


def band(depth):
    apart = jnp.abs(
        lax.broadcasted_iota(jnp.int32, (depth, depth), 0) - lax.broadcasted_iota(jnp.int32, (depth, depth), 1)
    )
    whole = jnp.zeros((depth, depth), jnp.float32)
    for j in range(1, WIDTH + 1):
        whole = jnp.where(apart == j, coefs[j], whole)
    high, low = split(whole, 2)
    return jnp.concatenate(
        [jnp.concatenate([high, low], axis=1), jnp.concatenate([high, jnp.zeros_like(high)], axis=1)], axis=0
    )


def split(value, terms):
    parts = []
    for _ in range(terms):
        part = value.astype(jnp.bfloat16)
        parts.append(part)
        value = value - part.astype(jnp.float32)
    return parts


def kernel(
    count, shots,
    courant, p_current, p_later, q_current, q_later, wavelet, source, receivers, residual,
    gradient, q_final,
    p_ext, q_ext, speed2, grad, spot, inject, others, matrix, summed,
    load_sem, out_sem, send_sem, recv_sem, share_send, share_recv,
):
    rows, ny, nz = speed2.shape
    me = lax.axis_index("space")
    shot = lax.axis_index("shot")
    odd = lax.rem(me, 2)
    exts = (p_ext, q_ext)
    currents = (p_current, q_current)
    ys = pl.ds(PAD, ny)

    def neighbour(side):
        return me - 1 + 2 * side

    def exists(side):
        return jnp.logical_and(neighbour(side) >= 0, neighbour(side) < count)

    def halo_copy(f, k, side):
        dst = exts[f].at[k + 1, pl.ds((1 - side) * (rows + WIDTH), WIDTH), ys]
        if isinstance(k, int) and k == 0:
            src = currents[f].at[0, pl.ds(side * (rows - WIDTH), WIDTH)]
        else:
            src = exts[f].at[k + 1, pl.ds(WIDTH + side * (rows - WIDTH), WIDTH), ys]
        return pltpu.make_async_remote_copy(
            src_ref=src, dst_ref=dst,
            send_sem=send_sem.at[f, k, side], recv_sem=recv_sem.at[f, k, side],
            device_id={"space": neighbour(side)}, device_id_type=pl.DeviceIdType.MESH,
        )

    def halo_wait(f, k, side):
        @pl.when(exists(side))
        def _():
            here = exts[f].at[k + 1, pl.ds(side * (rows + WIDTH), WIDTH), ys]
            pltpu.make_async_remote_copy(
                src_ref=here, dst_ref=here,
                send_sem=send_sem.at[f, k, 1 - side], recv_sem=recv_sem.at[f, k, 1 - side],
                device_id={"space": neighbour(side)}, device_id_type=pl.DeviceIdType.MESH,
            ).wait_recv()

    def halo_send(f, k, side):
        @pl.when(exists(side))
        def _():
            halo_copy(f, k, side).start()

    slow, fast = odd, 1 - odd

    loads = [
        pltpu.make_async_copy(courant, speed2, load_sem.at[0]),
        pltpu.make_async_copy(p_current.at[0], p_ext.at[1, pl.ds(WIDTH, rows), ys], load_sem.at[1]),
        pltpu.make_async_copy(q_current.at[0], q_ext.at[1, pl.ds(WIDTH, rows), ys], load_sem.at[2]),
        pltpu.make_async_copy(p_later.at[0], p_ext.at[0, pl.ds(WIDTH, rows), ys], load_sem.at[3]),
        pltpu.make_async_copy(q_later.at[0], q_ext.at[0, pl.ds(WIDTH, rows), ys], load_sem.at[4]),
    ]
    for load in loads:
        load.start()

    barrier = pltpu.get_barrier_semaphore()
    for side in (0, 1):
        @pl.when(exists(side))
        def _():
            pl.semaphore_signal(
                barrier, inc=1, device_id={"space": neighbour(side)}, device_id_type=pl.DeviceIdType.MESH
            )
    for d in range(1, shots):
        pl.semaphore_signal(
            barrier, inc=1, device_id={"shot": lax.rem(shot + d, shots)}, device_id_type=pl.DeviceIdType.MESH
        )
    pl.semaphore_wait(
        barrier, exists(0).astype(jnp.int32) + exists(1).astype(jnp.int32) + (shots - 1)
    )
    for f in (0, 1):
        for side in (slow, fast):
            halo_send(f, 0, side)

    matrix[...] = band(nz)
    for ext in exts:
        edge = jnp.zeros((ext.shape[0] - 1, rows, PAD, nz), jnp.float32)
        ext[1:, WIDTH:WIDTH + rows, 0:PAD, :] = edge
        ext[1:, WIDTH:WIDTH + rows, PAD + ny:PAD + ny + PAD, :] = edge
        outside = jnp.zeros((ext.shape[0] - 1, WIDTH, ny, nz), jnp.float32)
        for side in (0, 1):
            @pl.when(jnp.logical_not(exists(side)))
            def _():
                ext[1:, side * (rows + WIDTH):side * (rows + WIDTH) + WIDTH, PAD:PAD + ny, :] = outside

    shift = nz.bit_length() - 1
    cells = receivers[...]
    cell_row = lax.shift_right_logical(cells, shift) - me * (rows * ny)
    cell_column = jnp.bitwise_and(cells, nz - 1)
    column_hit = lax.broadcasted_iota(jnp.int32, (nz, cells.shape[1]), 0) == cell_column
    values = jnp.concatenate(
        [jnp.where(column_hit, residual[k], 0.0) for k in range(STEPS)], axis=0
    )
    value_parts = split(values, 3)
    block = WIDTH * ny
    for c in range(rows // WIDTH):
        ids = lax.broadcasted_iota(jnp.int32, (block, cells.shape[1]), 0) + c * block
        row_hit = jnp.where(ids == cell_row, 1.0, 0.0).astype(jnp.bfloat16)
        total = None
        for part in value_parts:
            term = lax.dot_general(
                row_hit, part, (((1,), (1,)), ((), ())), preferred_element_type=jnp.float32
            )
            total = term if total is None else total + term
        for k in range(STEPS):
            inject[k, c * WIDTH:(c + 1) * WIDTH] = total[:, k * nz:(k + 1) * nz].reshape(WIDTH, ny, nz)
        flat = (
            (lax.broadcasted_iota(jnp.int32, (WIDTH, ny, nz), 0) + (me * rows + c * WIDTH)) * (ny * nz)
            + lax.broadcasted_iota(jnp.int32, (WIDTH, ny, nz), 1) * nz
            + lax.broadcasted_iota(jnp.int32, (WIDTH, ny, nz), 2)
        )
        spot[c * WIDTH:(c + 1) * WIDTH] = jnp.where(flat == source[0], 1.0, 0.0)
    grad[...] = jnp.zeros_like(grad)
    for load in loads:
        load.wait()
    speed2[...] = speed2[...] * speed2[...]

    def laplace(ext, t, r0):
        here = pl.ds(r0 + WIDTH, WIDTH)
        core = ext[t, here, ys, :]
        pair = jnp.concatenate(split(core, 2), axis=-1).reshape(WIDTH * ny, 2 * nz)
        along_z = jnp.dot(pair, matrix[...], preferred_element_type=jnp.float32)
        total = (along_z[:, :nz] + along_z[:, nz:]).reshape(WIDTH, ny, nz) + 3.0 * coefs[0] * core
        for j in range(1, WIDTH + 1):
            total = total + coefs[j] * (
                (ext[t, pl.ds(r0 + WIDTH + j, WIDTH), ys, :] + ext[t, pl.ds(r0 + WIDTH - j, WIDTH), ys, :])
                + (ext[t, here, pl.ds(PAD + j, ny), :] + ext[t, here, pl.ds(PAD - j, ny), :])
            )
        return core, total

    def p_chunk(k, r0, last):
        core, lap = laplace(p_ext, k + 1, r0)
        own, here = pl.ds(r0, WIDTH), pl.ds(r0 + WIDTH, WIDTH)
        grad[own] += q_ext[k + 1, here, ys, :] * lap
        if not last:
            p_ext[k + 2, here, ys, :] = (
                2.0 * core - p_ext[k, here, ys, :] + speed2[own] * lap + wavelet[0, k] * spot[own]
            )

    def result_copy(r0):
        return pltpu.make_async_copy(
            q_ext.at[STEPS + 1, pl.ds(r0 + WIDTH, WIDTH), ys],
            q_final.at[0, pl.ds(r0, WIDTH)],
            out_sem.at[r0 // WIDTH],
        )

    def q_chunk(k, r0, last):
        core, lap = laplace(q_ext, k + 1, r0)
        own, here = pl.ds(r0, WIDTH), pl.ds(r0 + WIDTH, WIDTH)
        new = 2.0 * core - q_ext[k, here, ys, :] + speed2[own] * lap + inject[k, own]
        q_ext[k + 2, here, ys, :] = new
        if last:
            result_copy(r0).start()

    chunks = (p_chunk, q_chunk)

    def step(k, last=False, after_inner=None, after_side=None):
        for f in (0, 1):
            for c in range(1, rows // WIDTH - 1):
                chunks[f](k, c * WIDTH, last)
            if f == 0 and after_inner is not None:
                after_inner()
            for side in (slow, fast):
                halo_wait(f, k, side)
                chunks[f](k, side * (rows - WIDTH), last)
                if not last:
                    halo_send(f, k + 1, side)
                elif f == 0:
                    after_side(side)

    def loop(k, carry):
        step(k)
        return carry

    lax.fori_loop(0, STEPS - 1, loop, 0)

    share = ny // shots

    def share_copy(d, part, start, length):
        target = lax.rem(shot + d, shots)
        return pltpu.make_async_remote_copy(
            src_ref=grad.at[pl.ds(start, length), pl.ds(pl.multiple_of(target * share, share), share)],
            dst_ref=others.at[d - 1, pl.ds(start, length)],
            send_sem=share_send.at[d - 1, part], recv_sem=share_recv.at[d - 1, part],
            device_id={"shot": target}, device_id_type=pl.DeviceIdType.MESH,
        )

    def inner_parts(d):
        return share_copy(d, 2, WIDTH, rows - 2 * WIDTH)

    def side_part(d, side):
        return share_copy(d, side, side * (rows - WIDTH), WIDTH)

    def send_inner():
        for d in range(1, shots):
            inner_parts(d).start()

    def send_side(side):
        for d in range(1, shots):
            side_part(d, side).start()

    step(STEPS - 1, True, send_inner, send_side)

    for d in range(1, shots):
        inner_parts(d).wait()
        for side in (fast, slow):
            side_part(d, side).wait()
    total = grad[:, pl.ds(pl.multiple_of(shot * share, share), share), :]
    for d in range(1, shots):
        total = total + others[d - 1]
    summed[...] = total * (1.0 / (STEPS * shots))
    gradient_copy = pltpu.make_async_copy(summed, gradient, load_sem.at[0])
    gradient_copy.start()

    for f in (0, 1):
        for side in (0, 1):
            @pl.when(exists(side))
            def _():
                halo_copy(f, 0, side).wait_send()

                def finish(k, carry):
                    halo_copy(f, k, side).wait_send()
                    return carry

                lax.fori_loop(1, STEPS, finish, 0)

    for c in range(rows // WIDTH):
        result_copy(c * WIDTH).wait()
    gradient_copy.wait()


def body(courant, p_current, p_later, q_current, q_later, wavelet, source_cell, receiver_cells, residual_data):
    rows, ny, nz = courant.shape
    count, shots = lax.axis_size("space"), lax.axis_size("shot")
    share = ny // shots
    hbm = pl.BlockSpec(memory_space=pltpu.HBM)
    vmem = pl.BlockSpec(memory_space=pltpu.VMEM)
    smem = pl.BlockSpec(memory_space=pltpu.SMEM)
    cells = rows * ny * nz
    call = pl.pallas_call(
        functools.partial(kernel, count, shots),
        out_shape=(
            jax.ShapeDtypeStruct((rows, share, nz), jnp.float32),
            jax.ShapeDtypeStruct((1, rows, ny, nz), jnp.float32),
        ),
        in_specs=[hbm] * 5 + [smem, smem, vmem, vmem],
        out_specs=(hbm, hbm),
        scratch_shapes=[
            pltpu.VMEM((STEPS + 1, rows + 2 * WIDTH, ny + 2 * PAD, nz), jnp.float32),
            pltpu.VMEM((STEPS + 2, rows + 2 * WIDTH, ny + 2 * PAD, nz), jnp.float32),
            pltpu.VMEM((rows, ny, nz), jnp.float32),
            pltpu.VMEM((rows, ny, nz), jnp.float32),
            pltpu.VMEM((rows, ny, nz), jnp.float32),
            pltpu.VMEM((STEPS, rows, ny, nz), jnp.float32),
            pltpu.VMEM((max(shots - 1, 1), rows, share, nz), jnp.float32),
            pltpu.VMEM((2 * nz, 2 * nz), jnp.bfloat16),
            pltpu.VMEM((rows, share, nz), jnp.float32),
            pltpu.SemaphoreType.DMA((5,)),
            pltpu.SemaphoreType.DMA((rows // WIDTH,)),
            pltpu.SemaphoreType.DMA((2, STEPS, 2)),
            pltpu.SemaphoreType.DMA((2, STEPS, 2)),
            pltpu.SemaphoreType.DMA((max(shots - 1, 1), 3)),
            pltpu.SemaphoreType.DMA((max(shots - 1, 1), 3)),
        ],
        compiler_params=pltpu.CompilerParams(
            collective_id=0, has_side_effects=True, vmem_limit_bytes=60 * 1024 * 1024
        ),
        cost_estimate=pl.CostEstimate(
            flops=2 * STEPS * 40 * cells, bytes_accessed=7 * 4 * cells, transcendentals=0
        ),
    )
    return call(
        courant, p_current, p_later, q_current, q_later, wavelet, source_cell, receiver_cells,
        jnp.swapaxes(residual_data, 0, 1),
    )


def solution(mesh):
    in_specs = (
        P("space", None, None),
        P("shot", "space", None, None),
        P("shot", "space", None, None),
        P("shot", "space", None, None),
        P("shot", "space", None, None),
        P("shot", None),
        P("shot"),
        P("shot", None),
        P("shot", None, None),
    )
    out_specs = (P("space", "shot", None), P("shot", "space", None, None))
    return jax.shard_map(body, mesh=mesh, in_specs=in_specs, out_specs=out_specs, check_vma=False)
```
